512 devices in a mesh: gx: 32 (over x, y), yz: 16 (over z, core).
Axes of the slice: x: 4, y: 8, z: 8, core: 2. Of those that a mesh axis runs over, the one named last changes fastest.
Arguments:
- state: float32 [27, 128, 128, 128], P(None, 'gx', 'yz'), may hold values from -6 to 6
- mix_weights: float32 [32, 16, 4, 27, 1024], P('gx', 'yz'), may hold values from -6 to 6
- mix_frac: float32 [32, 16, 4, 1024], P('gx', 'yz'), as said below
- mix_index: int32 [32, 16, 1024], P('gx', 'yz'), may hold values from 0 to 4095, as said below
- mix_count: int32 [32, 16], P('gx', 'yz'), may hold values from 128 to 1024, as said below
- vol_matrix: float32 [27, 27], replicated, may hold values from -0.6 to 0.6
- face_matrix: float32 [27, 54], replicated, may hold values from -0.5 to 0.5
- mat_matrix: float32 [4, 27, 27], replicated, may hold values from -0.6 to 0.6
Outputs:
- field: float32 [27, 128, 128, 128], P(None, 'gx', 'yz')
- weights_out: float32 [32, 16, 4, 27, 1024], P('gx', 'yz')
The draws below stay inside these ranges and needn't reach their ends.
Inputs may be any that keep to these rules, and one draw needn't show every extreme that they name: `mix_index`: within one device's list the entries are distinct zone numbers of that device's block. `mix_count`: one device has 1024 live slots and another 1024 // 8. `mix_frac`: Positive; the 4 fractions of a slot sum to one.
All inputs are finite; a program needn't handle non-finite values.
Results may differ from the reference program's by a relative error of at most 0.0001.
Values sent between devices are 32-bit elements; how exact they have to be, the bound alone decides.
No kernel may reach another device: no remote copies, remote signals or barrier semaphores. Data moves between devices by JAX's collectives and lax.ppermute only.
A program may use at most 128 MiB of HBM per device.

```python
import jax
import jax.numpy as jnp
from jax import lax

DOFS = 27
MAT = 4
SWEEPS = 4
CX = 4
CY = 8
CZ = 128
MIX_CAP = 1024
NX = 128
NY = 128
NZ = 128
N_GX = 32
N_YZ = 16


def draw_mix_count(key, part):
    key = jax.random.fold_in(key, 11)
    first_key, second_key, third_key = jax.random.split(key, 3)
    devices_all = N_GX * N_YZ
    counts = jax.random.randint(first_key, (devices_all,), MIX_CAP // 8, MIX_CAP // 2 + 1)
    busiest = jax.random.randint(second_key, (), 0, devices_all)
    lightest = (busiest + 1 + jax.random.randint(third_key, (), 0, devices_all - 1)) % devices_all
    position = jnp.arange(devices_all)
    counts = jnp.where(position == busiest, MIX_CAP, jnp.where(position == lightest, MIX_CAP // 8, counts))
    return counts.reshape(N_GX, N_YZ).astype(jnp.int32)


def draw_mix_index(key, part):
    key = jax.random.fold_in(key, 12)
    keys = jax.random.split(key, N_GX * N_YZ)
    lists = jax.vmap(lambda one_key: jax.random.permutation(one_key, CX * CY * CZ)[:MIX_CAP])(keys)
    return lists.reshape(N_GX, N_YZ, MIX_CAP).astype(jnp.int32)


def draw_mix_frac(key, part):
    key = jax.random.fold_in(key, 13)
    raw = jnp.exp(jax.random.uniform(key, (N_GX, N_YZ, MAT, MIX_CAP), jnp.float32, -1.5, 1.5))
    return raw / jnp.sum(raw, axis=2, keepdims=True)


def levels(key, extent, shards, smallest, top_value):
    level = 1.0
    for dim, blocks in shards:
        draws = jax.random.uniform(jax.random.fold_in(jax.random.fold_in(key, 6), dim), (blocks,), jnp.float32, smallest / len(shards), top_value / len(shards))
        level = level * jnp.repeat(jnp.exp(draws), extent[dim] // blocks).reshape((-1,) + (1,) * (len(extent) - 1 - dim))
    return level


def bell_draw(rng, dims, width, most, shards=(), held_as=jnp.bfloat16):
    array = jax.random.normal(rng, dims, jnp.float32) * width
    if len(shards) > 0:
        array = levels(rng, dims, shards, -0.22, 0.18) * array
    return jnp.clip(array, min=-most, max=most).astype(held_as)


def setup_inputs(seed: int = 0) -> dict:
    key_of = jax.random.split(jax.random.key(seed), 9)
    return {
        "state": bell_draw(key_of[0], (DOFS, NX, NY, NZ), 1.0, 6.0, ((1, 32), (2, 16)), jnp.float32),
        "mix_weights": bell_draw(key_of[1], (N_GX, N_YZ, MAT, DOFS, MIX_CAP), 1.0, 6.0, ((0, 32), (1, 16)), jnp.float32),
        "mix_frac": draw_mix_frac(jax.random.fold_in(key_of[8], 71), 0),
        "mix_index": draw_mix_index(jax.random.fold_in(key_of[8], 71), 0),
        "mix_count": draw_mix_count(jax.random.fold_in(key_of[8], 71), 0),
        "vol_matrix": bell_draw(key_of[5], (DOFS, DOFS), 0.1, 0.6, (), jnp.float32),
        "face_matrix": bell_draw(key_of[6], (DOFS, 6 * 9), 0.08, 0.5, (), jnp.float32),
        "mat_matrix": bell_draw(key_of[7], (MAT, DOFS, DOFS), 0.1, 0.6, (), jnp.float32),
    }


highest = lax.Precision.HIGHEST
SECTIONS = ((0.0, 1.0), (0.75, 0.25), (1.0 / 3.0, 2.0 / 3.0))


def face_rates(field, padded, volume, lifting):
    nx_cells, ny_cells, nz_cells = field.shape[1], field.shape[2], field.shape[3]
    lattice = field.reshape(3, 3, 3, nx_cells, ny_cells, nz_cells)

    def beside(shift_x, shift_y):
        return padded[:, shift_x:shift_x + nx_cells, shift_y:shift_y + ny_cells].reshape(3, 3, 3, nx_cells, ny_cells, nz_cells)

    zeros_rim = jnp.zeros((3, 3, nx_cells, ny_cells, 1), field.dtype)
    below_z = jnp.concatenate([zeros_rim, lattice[:, :, 2, :, :, :-1]], axis=-1)
    above_z = jnp.concatenate([lattice[:, :, 0, :, :, 1:], zeros_rim], axis=-1)
    jumps = [beside(0, 1)[2] - lattice[0], beside(2, 1)[0] - lattice[2],
             beside(1, 0)[:, 2] - lattice[:, 0], beside(1, 2)[:, 0] - lattice[:, 2],
             below_z - lattice[:, :, 0], above_z - lattice[:, :, 2]]
    stacked = jnp.concatenate([jump.reshape(9, -1) for jump in jumps], axis=0)
    return jnp.dot(volume, field.reshape(27, -1), precision=highest) + jnp.dot(lifting, stacked, precision=highest)


def sweep_rates(weights_now, resid, mat_matrix):
    iterate = weights_now
    for sweep in range(SWEEPS):
        iterate = weights_now + jnp.einsum('mpq,mqs->mps', mat_matrix, iterate, precision=highest)
    return iterate - weights_now + resid[None]


def reference(state, mix_weights, mix_frac, mix_index, mix_count, vol_matrix, face_matrix, mat_matrix):
    slots = N_GX * N_YZ * MIX_CAP
    dev_x = jnp.arange(N_GX, dtype=jnp.int32)[:, None, None]
    dev_y = jnp.arange(N_YZ, dtype=jnp.int32)[None, :, None]
    local_x = mix_index // (CY * CZ)
    local_y = (mix_index // CZ) % CY
    local_z = mix_index % CZ
    zone_ids = (((dev_x * CX + local_x) * NY + dev_y * CY + local_y) * NZ + local_z).reshape(slots).astype(jnp.int32)
    live = (jnp.arange(MIX_CAP, dtype=jnp.int32)[None, None, :] < mix_count[:, :, None]).reshape(slots)
    w_start = jnp.transpose(mix_weights, (2, 3, 0, 1, 4)).reshape(MAT, DOFS, slots)
    fractions = jnp.transpose(mix_frac, (2, 0, 1, 3)).reshape(MAT, slots)
    field = state
    w_now = w_start
    for old_part, new_part in SECTIONS:
        padded = jnp.pad(field, ((0, 0), (1, 1), (1, 1), (0, 0)))
        rate = face_rates(field, padded, vol_matrix, face_matrix)
        resid = jnp.take(rate, zone_ids, axis=1)
        rate_w = jnp.where(live[None, None], sweep_rates(w_now, resid, mat_matrix), 0.0)
        w_next = old_part * w_start + new_part * (w_now + rate_w)
        field = old_part * state + new_part * (field + rate.reshape(state.shape))
        closure = jnp.sum(fractions[:, None, :] * w_next, axis=0)
        flat_field = field.reshape(DOFS, -1)
        current = jnp.take(flat_field, zone_ids, axis=1)
        flat_field = flat_field.at[:, zone_ids].set(jnp.where(live[None], closure, current))
        field = flat_field.reshape(state.shape)
        w_now = w_next
    weights_out = jnp.transpose(w_now.reshape(MAT, DOFS, N_GX, N_YZ, MIX_CAP), (2, 3, 0, 1, 4))
    return field, weights_out
```

```python
import numpy as np
import jax
import jax.numpy as jnp
from jax import lax
from jax.experimental import pallas as pl
from jax.experimental.pallas import tpu as pltpu
from jax.sharding import PartitionSpec as P

F32 = jnp.float32
BF16 = jnp.bfloat16
CX, CY, CZ = 4, 8, 128
ROWS = CX * CY
ZONES = ROWS * CZ
SLOTS = 1024
GROUP = 256
GROUPS = ZONES // GROUP
HIGHEST = lax.Precision.HIGHEST


def face_dofs(face, own):
    axis, high = divmod(face, 2)
    at = (2 if high else 0) if own else (0 if high else 2)
    dofs = []
    for p in range(3):
        for q in range(3):
            abc = [p, q]
            abc.insert(axis, at)
            dofs.append(abc[0] * 9 + abc[1] * 3 + abc[2])
    return dofs


def selections():
    sel = np.zeros((64, 7 * 128 + 4 * 64), np.float32)
    for face in range(6):
        for q in range(9):
            row = 9 * face + q
            for copy in range(4):
                sel[row, copy * 32 + face_dofs(face, True)[q]] -= 1.0
                sel[row, (face + 1) * 128 + copy * 32 + face_dofs(face, False)[q]] += 1.0
                if face < 4:
                    sel[row, 7 * 128 + face * 64 + copy * 16 + q] += 1.0
    return sel


def halves(x):
    hi = x.astype(BF16)
    lo = (x - hi.astype(F32)).astype(BF16)
    return hi, lo


def stack_right(x):
    hi, lo = halves(x)
    return jnp.concatenate([hi, lo, hi, lo], axis=0)


def stack_left(x, half):
    hi = x.astype(BF16).astype(F32)
    lane = lax.broadcasted_iota(jnp.int32, x.shape, 1)
    return jnp.where(lane < half, hi, x - hi).astype(BF16)


def dot(a, b):
    return jnp.dot(a, b, preferred_element_type=F32)


def block(r):
    return slice(r * CZ, (r + 1) * CZ)


def interior(v_ref, wg_ref, g_ref, out_ref):
    for x in range(CX):
        cols = slice(x * 1024, (x + 1) * 1024)
        g_ref[:, cols] = dot(wg_ref[...], stack_right(v_ref[:, cols]))
    lane = lax.broadcasted_iota(jnp.int32, (32, CZ), 1)
    for x in range(CX):
        for y in range(CY):
            r = x * CY + y
            total = g_ref[0:32, block(r)]
            if x > 0:
                total += g_ref[32:64, block(r - CY)]
            if x < CX - 1:
                total += g_ref[64:96, block(r + CY)]
            if y > 0:
                total += g_ref[96:128, block(r - 1)]
            if y < CY - 1:
                total += g_ref[128:160, block(r + 1)]
            below = pltpu.roll(g_ref[160:192, block(r)], 1, 1)
            above = pltpu.roll(g_ref[192:224, block(r)], CZ - 1, 1)
            total += jnp.where(lane == 0, 0.0, below)
            total += jnp.where(lane == CZ - 1, 0.0, above)
            out_ref[:, block(r)] = total


def lane_hot(idx):
    place = lax.broadcasted_iota(jnp.int32, (GROUP, SLOTS), 0)
    return jnp.where(place == (idx & (GROUP - 1)), 1.0, 0.0).astype(BF16)


def to_slots(r_ref, hot, idx):
    total = jnp.zeros((32, SLOTS), F32)
    group = lax.shift_right_logical(idx, 8)
    for g in range(GROUPS):
        hi, lo = halves(r_ref[:, g * GROUP:(g + 1) * GROUP])
        both = dot(jnp.concatenate([hi, lo], axis=0), hot)
        total = jnp.where(group == g, both[0:32] + both[32:64], total)
    return total


def first_kernel(state_ref, v_ref, xlo_ref, xhi_ref, ylo_ref, yhi_ref):
    for q in range(9):
        xlo_ref[q * 8:q * 8 + 8, :] = state_ref[q * 32:q * 32 + 8, :]
        xhi_ref[q * 8:q * 8 + 8, :] = state_ref[(18 + q) * 32 + 24:(18 + q) * 32 + 32, :]
        low, high = face_dofs(2, True)[q], face_dofs(3, True)[q]
        ylo_ref[q * 4:q * 4 + 4, :] = state_ref[pl.ds(low * 32, 4, stride=8), :]
        yhi_ref[q * 4:q * 4 + 4, :] = state_ref[pl.ds(high * 32 + 7, 4, stride=8), :]
    v_ref[24:32, :] = jnp.zeros((8, ZONES), F32)
    for r in range(ROWS):
        v_ref[0:27, block(r)] = state_ref[pl.ds(r, 27, stride=32), :]


def mixed_kernel(
    count_ref, v_ref, w_ref, frac_ref, idx_ref, vol_ref, face_ref, mat_ref, sel_ref,
    int_ref, u_ref, c2_ref, c3_ref, fm_ref, wg_ref, fh_ref, pp_ref, b3_ref,
    g_ref, small_ref, diag_ref, wpad_ref, c_ref,
):
    small_ref[...] = jnp.zeros((32, 128), F32)
    small_ref[0:27, 0:54] = face_ref[...]
    f_hi, f_lo = halves(small_ref[:, 0:64])
    laid = dot(f_hi, sel_ref[...]) + dot(f_lo, sel_ref[...])
    small_ref[...] = jnp.zeros((32, 128), F32)
    small_ref[0:27, 0:27] = vol_ref[...]
    vol = small_ref[...]
    vol4 = vol + pltpu.roll(vol, 32, 1)
    vol4 = vol4 + pltpu.roll(vol4, 64, 1)
    wg_ref[0:32, :] = stack_left(laid[:, 0:128] + vol4, 64)
    for k in range(1, 7):
        wg_ref[32 * k:32 * k + 32, :] = stack_left(laid[:, 128 * k:128 * k + 128], 64)
    for k in range(4):
        first = 7 * 128 + 64 * k
        fh_ref[32 * k:32 * k + 32, :] = stack_left(laid[:, first:first + 64], 32)
    interior(v_ref, wg_ref, g_ref, int_ref)

    for m in range(4):
        small_ref[0:27, 0:27] = mat_ref[m]
        small = small_ref[...]
        diag_ref[32 * m:32 * m + 32, :] = pltpu.roll(small, 32 * m, 1) if m else small
    m1 = diag_ref[...]
    row = lax.broadcasted_iota(jnp.int32, (128, 128), 0)
    column = lax.broadcasted_iota(jnp.int32, (128, 128), 1)
    eye = jnp.where(row == column, 1.0, 0.0)
    m2 = jnp.dot(m1, m1, precision=HIGHEST)
    p1 = eye + m1 + m2 + jnp.dot(m1 + m2, m2, precision=HIGHEST)
    p2 = jnp.dot(p1, p1, precision=HIGHEST)
    p3 = jnp.dot(p2, p1, precision=HIGHEST)
    q2 = 0.75 * eye + 0.25 * p2
    q3 = (1.0 / 3.0) * eye + 0.5 * p1 + (1.0 / 6.0) * p3

    def stacked(matrix, m):
        rows = matrix[32 * m:32 * m + 32, :]
        for shift in (32, 64):
            rows = rows + pltpu.roll(rows, shift, 1)
        return stack_left(rows, 64)

    for m in range(4):
        pp_ref[32 * m:32 * m + 32, :] = stacked(p1, m)
        pp_ref[128 + 32 * m:128 + 32 * m + 32, :] = stacked(p2, m)

    idx = idx_ref[...]
    slot = lax.broadcasted_iota(jnp.int32, (1, SLOTS), 1)
    live = slot < count_ref[0, 0]
    frac = frac_ref[...]
    c_ref[...] = jnp.zeros((112, SLOTS), F32)
    wpad_ref[...] = jnp.zeros((32, SLOTS), F32)
    sums = [0.0, 0.0, 0.0]
    for m in range(4):
        wpad_ref[0:27, :] = w_ref[m]
        left = jnp.concatenate([stacked(p1, m), stacked(q2, m), stacked(q3, m)], axis=0)
        values = dot(left, stack_right(wpad_ref[...]))
        for k in range(3):
            sums[k] = sums[k] + frac[m:m + 1, :] * values[32 * k:32 * k + 32]
        b3_ref[m] = values[64:96]
    for k in range(3):
        c_ref[32 * k:32 * k + 32, :] = jnp.where(live, sums[k], 0.0)
    c_ref[96:100, :] = jnp.where(live, frac, 0.0)
    c_ref[100:101, :] = jnp.where(live, 1.0, 0.0)

    hot = lane_hot(idx)
    group = lax.shift_right_logical(idx, 8)
    hi, lo = halves(c_ref[...])
    both = jnp.concatenate([hi, lo], axis=0)
    for g in range(GROUPS):
        cols = slice(g * GROUP, (g + 1) * GROUP)
        here = jnp.where(group == g, 1.0, 0.0).astype(BF16)
        dense = lax.dot_general(
            both * here, hot, (((1,), (1,)), ((), ())), preferred_element_type=F32
        )
        dense = dense[0:112] + dense[112:224]
        u_ref[:, cols] = jnp.where(dense[100:101] > 0.5, dense[0:32], v_ref[:, cols])
        c2_ref[:, cols] = dense[32:64]
        c3_ref[:, cols] = dense[64:96]
        fm_ref[:, cols] = dense[96:104]


def halo_add(int_ref, fh_ref, xlo_ref, xhi_ref, ylo_ref, yhi_ref, pad_ref, rate_ref):
    pad_ref[...] = jnp.zeros((16, 3072), F32)
    for y in range(CY):
        pad_ref[0:9, block(y)] = xlo_ref[pl.ds(y, 9, stride=8), :]
        pad_ref[0:9, block(CY + y)] = xhi_ref[pl.ds(y, 9, stride=8), :]
    for x in range(CX):
        pad_ref[0:9, block(16 + x)] = ylo_ref[pl.ds(x, 9, stride=4), :]
        pad_ref[0:9, block(20 + x)] = yhi_ref[pl.ds(x, 9, stride=4), :]
    x_low = dot(fh_ref[0:32, :], stack_right(pad_ref[:, 0:1024]))
    x_high = dot(fh_ref[32:64, :], stack_right(pad_ref[:, 1024:2048]))
    y_low = dot(fh_ref[64:96, :], stack_right(pad_ref[:, 2048:2560]))
    y_high = dot(fh_ref[96:128, :], stack_right(pad_ref[:, 2560:3072]))
    for x in range(CX):
        for y in range(CY):
            r = x * CY + y
            total = int_ref[:, block(r)]
            if x == 0:
                total += x_low[:, block(y)]
            if x == CX - 1:
                total += x_high[:, block(y)]
            if y == 0:
                total += y_low[:, block(x)]
            if y == CY - 1:
                total += y_high[:, block(x)]
            rate_ref[:, block(r)] = total


def step_kernel(
    part, int_ref, u_ref, fh_ref, xl_ref, xh_ref, yl_ref, yh_ref,
    v_ref, rate_ref, xlo_ref, xhi_ref, ylo_ref, yhi_ref, pad_ref,
):
    halo_add(int_ref, fh_ref, xl_ref, xh_ref, yl_ref, yh_ref, pad_ref, rate_ref)
    v_ref[...] = u_ref[...] + part * rate_ref[...]
    for y in range(CY):
        xlo_ref[pl.ds(y, 9, stride=8), :] = v_ref[0:9, block(y)]
        xhi_ref[pl.ds(y, 9, stride=8), :] = v_ref[18:27, block(24 + y)]
    for x in range(CX):
        for a in range(3):
            ylo_ref[pl.ds(12 * a + x, 3, stride=4), :] = v_ref[9 * a:9 * a + 3, block(8 * x)]
            yhi_ref[pl.ds(12 * a + x, 3, stride=4), :] = v_ref[9 * a + 6:9 * a + 9, block(8 * x + 7)]


def between_one(
    v0_ref, v1_ref, r_ref, c2_ref, c3_ref, fm_ref, idx_ref, wg_ref, pp_ref, b3_ref,
    int_ref, u_ref, c3_out, b3_out, g_ref,
):
    interior(v1_ref, wg_ref, g_ref, int_ref)
    for x in range(CX):
        cols = slice(x * 1024, (x + 1) * 1024)
        q = dot(pp_ref[...], stack_right(r_ref[:, cols]))
        f = fm_ref[:, cols]
        s1 = sum(f[m:m + 1] * q[32 * m:32 * m + 32] for m in range(4))
        s2 = sum(f[m:m + 1] * q[128 + 32 * m:160 + 32 * m] for m in range(4))
        bulk = 0.75 * v0_ref[:, cols] + 0.25 * v1_ref[:, cols]
        u_ref[:, cols] = jnp.where(f[4:5] > 0.5, c2_ref[:, cols] + 0.25 * s1, bulk)
        c3_out[:, cols] = c3_ref[:, cols] + (1.0 / 6.0) * s2
    idx = idx_ref[...]
    at = stack_right(to_slots(r_ref, lane_hot(idx), idx))
    for m in range(4):
        b3_out[m] = b3_ref[m] + (1.0 / 6.0) * dot(pp_ref[128 + 32 * m:160 + 32 * m, :], at)


def between_two(
    v0_ref, v2_ref, r_ref, c3_ref, fm_ref, idx_ref, wg_ref, pp_ref, b3_ref,
    int_ref, u_ref, b3_out, g_ref,
):
    interior(v2_ref, wg_ref, g_ref, int_ref)
    for x in range(CX):
        cols = slice(x * 1024, (x + 1) * 1024)
        q = dot(pp_ref[0:128, :], stack_right(r_ref[:, cols]))
        f = fm_ref[:, cols]
        s1 = sum(f[m:m + 1] * q[32 * m:32 * m + 32] for m in range(4))
        bulk = (1.0 / 3.0) * v0_ref[:, cols] + (2.0 / 3.0) * v2_ref[:, cols]
        u_ref[:, cols] = jnp.where(f[4:5] > 0.5, c3_ref[:, cols] + (1.0 / 6.0) * s1, bulk)
    idx = idx_ref[...]
    at = stack_right(to_slots(r_ref, lane_hot(idx), idx))
    for m in range(4):
        b3_out[m] = b3_ref[m] + (1.0 / 6.0) * dot(pp_ref[32 * m:32 * m + 32, :], at)


def last_kernel(
    count_ref, int_ref, u_ref, fh_ref, xl_ref, xh_ref, yl_ref, yh_ref, idx_ref, b3_ref, w_ref,
    field_ref, out_ref, pad_ref, rate_ref,
):
    halo_add(int_ref, fh_ref, xl_ref, xh_ref, yl_ref, yh_ref, pad_ref, rate_ref)
    for r in range(ROWS):
        value = u_ref[0:27, block(r)] + (2.0 / 3.0) * rate_ref[0:27, block(r)]
        field_ref[pl.ds(r, 27, stride=32), :] = value
    idx = idx_ref[...]
    at = (2.0 / 3.0) * to_slots(rate_ref, lane_hot(idx), idx)
    live = lax.broadcasted_iota(jnp.int32, (1, SLOTS), 1) < count_ref[0, 0]
    for m in range(4):
        out_ref[m] = jnp.where(live, b3_ref[m, 0:27, :] + at[0:27], w_ref[m])


VMEM = pl.BlockSpec(memory_space=pltpu.VMEM)
SMEM = pl.BlockSpec(memory_space=pltpu.SMEM)
DENSE = jax.ShapeDtypeStruct((32, ZONES), F32)
FACES = [jax.ShapeDtypeStruct((72, 128), F32)] * 2 + [jax.ShapeDtypeStruct((36, 128), F32)] * 2
SLOT3 = jax.ShapeDtypeStruct((4, 32, SLOTS), F32)


def call(kernel, outs, args, scratch=(), smem=0, flops=0):
    specs = [SMEM] * smem + [VMEM] * (len(args) - smem)
    moved = 4 * sum(int(np.prod(a.shape)) for a in list(args) + list(outs))
    return pl.pallas_call(
        kernel,
        out_shape=outs,
        in_specs=specs,
        out_specs=[VMEM] * len(outs),
        scratch_shapes=list(scratch),
        compiler_params=pltpu.CompilerParams(vmem_limit_bytes=48 * 1024 * 1024),
        cost_estimate=pl.CostEstimate(flops=flops, bytes_accessed=moved, transcendentals=0),
    )(*args)


def exchange(faces):
    x_low, x_high, y_low, y_high = faces

    def neighbours(axis, low, high):
        up = [(i, i + 1) for i in range(lax.axis_size(axis) - 1)]
        down = [(j, i) for i, j in up]
        return lax.ppermute(high, axis, up), lax.ppermute(low, axis, down)

    return (*neighbours("gx", x_low, x_high), *neighbours("yz", y_low, y_high))


def on_device(
    state, mix_weights, mix_frac, mix_index, mix_count, vol_matrix, face_matrix, mat_matrix
):
    flat = state.reshape(27 * ROWS, CZ)
    weights = mix_weights.reshape(4, 27, SLOTS)
    frac = mix_frac.reshape(4, SLOTS)
    idx = mix_index.reshape(1, SLOTS)
    count = mix_count.reshape(1, 1)
    sel = jnp.asarray(selections(), BF16)
    g_space = pltpu.VMEM((224, ZONES), F32)
    pad = pltpu.VMEM((16, 3072), F32)

    v0, *faces = call(first_kernel, [DENSE] + FACES, [flat])
    halo = exchange(faces)
    bf = lambda rows, lanes: jax.ShapeDtypeStruct((rows, lanes), BF16)
    fm_shape = jax.ShapeDtypeStruct((8, ZONES), F32)
    inner, u, c2, c3, fm, wg, fh, pp, b3 = call(
        mixed_kernel,
        [DENSE, DENSE, DENSE, DENSE, fm_shape, bf(224, 128), bf(128, 64), bf(256, 128), SLOT3],
        [count, v0, weights, frac, idx, vol_matrix, face_matrix, mat_matrix, sel],
        [g_space, pltpu.VMEM((32, 128), F32), pltpu.VMEM((128, 128), F32),
         pltpu.VMEM((32, SLOTS), F32), pltpu.VMEM((112, SLOTS), F32)],
        smem=1, flops=4 * 10**9,
    )

    def step(part, inner, u, halo):
        def kernel(*refs):
            step_kernel(part, *refs)
        v, rate, *faces = call(kernel, [DENSE, DENSE] + FACES, [inner, u, fh, *halo], [pad])
        return v, rate, exchange(faces)

    v1, r0, halo = step(1.0, inner, u, halo)
    inner, u, c3, b3 = call(
        between_one, [DENSE, DENSE, DENSE, SLOT3],
        [v0, v1, r0, c2, c3, fm, idx, wg, pp, b3], [g_space], flops=2 * 10**9,
    )
    v2, r1, halo = step(0.25, inner, u, halo)
    inner, u, b3 = call(
        between_two, [DENSE, DENSE, SLOT3],
        [v0, v2, r1, c3, fm, idx, wg, pp, b3], [g_space], flops=2 * 10**9,
    )
    field, out = call(
        last_kernel,
        [jax.ShapeDtypeStruct((27 * ROWS, CZ), F32), jax.ShapeDtypeStruct((4, 27, SLOTS), F32)],
        [count, inner, u, fh, *halo, idx, b3, weights],
        [pad, pltpu.VMEM((32, ZONES), F32)], smem=1,
    )
    return field.reshape(state.shape), out.reshape(mix_weights.shape)


def solution(mesh):
    placed = (
        P(None, "gx", "yz", None),
        P("gx", "yz", None, None, None),
        P("gx", "yz", None, None),
        P("gx", "yz", None),
        P("gx", "yz"),
        P(),
        P(),
        P(),
    )
    return jax.shard_map(
        on_device,
        mesh=mesh,
        in_specs=placed,
        out_specs=(P(None, "gx", "yz", None), P("gx", "yz", None, None, None)),
        check_vma=False,
    )
```

```python
import numpy as np
import jax
import jax.numpy as jnp
from jax import lax
from jax.experimental import pallas as pl
from jax.experimental.pallas import tpu as pltpu
from jax.sharding import PartitionSpec as P

F32 = jnp.float32
BF16 = jnp.bfloat16
CX, CY, CZ = 4, 8, 128
ROWS = CX * CY
ZONES = ROWS * CZ
SLOTS = 1024
GROUP = 256
GROUPS = ZONES // GROUP
HIGHEST = lax.Precision.HIGHEST


def face_dofs(face, own):
    axis, high = divmod(face, 2)
    at = (2 if high else 0) if own else (0 if high else 2)
    dofs = []
    for p in range(3):
        for q in range(3):
            abc = [p, q]
            abc.insert(axis, at)
            dofs.append(abc[0] * 9 + abc[1] * 3 + abc[2])
    return dofs


def selections():
    sel = np.zeros((64, 7 * 128 + 4 * 64), np.float32)
    for face in range(6):
        for q in range(9):
            row = 9 * face + q
            for copy in range(4):
                sel[row, copy * 32 + face_dofs(face, True)[q]] -= 1.0
                sel[row, (face + 1) * 128 + copy * 32 + face_dofs(face, False)[q]] += 1.0
                if face < 4:
                    sel[row, 7 * 128 + face * 64 + copy * 16 + q] += 1.0
    return sel


def halves(x):
    hi = x.astype(BF16)
    lo = (x - hi.astype(F32)).astype(BF16)
    return hi, lo


def stack_right(x):
    hi, lo = halves(x)
    return jnp.concatenate([hi, lo, hi, lo], axis=0)


def stack_left(x, half):
    hi = x.astype(BF16).astype(F32)
    lane = lax.broadcasted_iota(jnp.int32, x.shape, 1)
    return jnp.where(lane < half, hi, x - hi).astype(BF16)


def dot(a, b):
    return jnp.dot(a, b, preferred_element_type=F32)


def block(r):
    return slice(r * CZ, (r + 1) * CZ)


def interior(v_ref, wg_ref, g_ref, out_ref):
    for x in range(CX):
        cols = slice(x * 1024, (x + 1) * 1024)
        g_ref[:, cols] = dot(wg_ref[...], stack_right(v_ref[:, cols]))
    lane = lax.broadcasted_iota(jnp.int32, (32, CZ), 1)
    for x in range(CX):
        for y in range(CY):
            r = x * CY + y
            total = g_ref[0:32, block(r)]
            if x > 0:
                total += g_ref[32:64, block(r - CY)]
            if x < CX - 1:
                total += g_ref[64:96, block(r + CY)]
            if y > 0:
                total += g_ref[96:128, block(r - 1)]
            if y < CY - 1:
                total += g_ref[128:160, block(r + 1)]
            below = pltpu.roll(g_ref[160:192, block(r)], 1, 1)
            above = pltpu.roll(g_ref[192:224, block(r)], CZ - 1, 1)
            total += jnp.where(lane == 0, 0.0, below)
            total += jnp.where(lane == CZ - 1, 0.0, above)
            out_ref[:, block(r)] = total


def lane_hot(idx):
    place = lax.broadcasted_iota(jnp.int32, (GROUP, SLOTS), 0)
    return jnp.where(place == (idx & (GROUP - 1)), 1.0, 0.0).astype(BF16)


def to_slots(r_ref, hot, idx):
    total = jnp.zeros((32, SLOTS), F32)
    group = lax.shift_right_logical(idx, 8)
    for g in range(GROUPS):
        hi, lo = halves(r_ref[:, g * GROUP:(g + 1) * GROUP])
        both = dot(jnp.concatenate([hi, lo], axis=0), hot)
        total = jnp.where(group == g, both[0:32] + both[32:64], total)
    return total


def first_kernel(*refs):
    count = 8
    sources, (v_ref, ylo_ref, yhi_ref), rest = refs[:count], refs[count:count + 3], refs[count + 3:]
    targets, (state_ref, sems) = rest[:count - 1], rest[count - 1:]
    copies = [
        pltpu.make_async_copy(source, target, sems.at[k])
        for k, (source, target) in enumerate(zip(sources, (state_ref,) + targets))
    ]
    for copy in copies:
        copy.start()
    v_ref[24:32, :] = jnp.zeros((8, ZONES), F32)
    copies[0].wait()
    for q in range(9):
        low, high = face_dofs(2, True)[q], face_dofs(3, True)[q]
        ylo_ref[q * 4:q * 4 + 4, :] = state_ref[pl.ds(low * 32, 4, stride=8), :]
        yhi_ref[q * 4:q * 4 + 4, :] = state_ref[pl.ds(high * 32 + 7, 4, stride=8), :]
    for r in range(ROWS):
        v_ref[0:27, block(r)] = state_ref[pl.ds(r, 27, stride=32), :]
    for copy in copies[1:]:
        copy.wait()


def mixed_kernel(
    count_ref, v_ref, w_ref, frac_ref, idx_ref, vol_ref, face_ref, mat_ref, sel_ref,
    int_ref, u_ref, fm_ref, wg_ref, fh_ref, pp_ref, b3_ref, c_ref,
    g_ref, small_ref, diag_ref, wpad_ref,
):
    small_ref[...] = jnp.zeros((32, 128), F32)
    small_ref[0:27, 0:54] = face_ref[...]
    f_hi, f_lo = halves(small_ref[:, 0:64])
    laid = dot(f_hi, sel_ref[...]) + dot(f_lo, sel_ref[...])
    small_ref[...] = jnp.zeros((32, 128), F32)
    small_ref[0:27, 0:27] = vol_ref[...]
    vol = small_ref[...]
    vol4 = vol + pltpu.roll(vol, 32, 1)
    vol4 = vol4 + pltpu.roll(vol4, 64, 1)
    wg_ref[0:32, :] = stack_left(laid[:, 0:128] + vol4, 64)
    for k in range(1, 7):
        wg_ref[32 * k:32 * k + 32, :] = stack_left(laid[:, 128 * k:128 * k + 128], 64)
    for k in range(4):
        first = 7 * 128 + 64 * k
        fh_ref[32 * k:32 * k + 32, :] = stack_left(laid[:, first:first + 64], 32)
    interior(v_ref, wg_ref, g_ref, int_ref)

    for m in range(4):
        small_ref[0:27, 0:27] = mat_ref[:, m, :]
        small = small_ref[...]
        diag_ref[32 * m:32 * m + 32, :] = pltpu.roll(small, 32 * m, 1) if m else small
    m1 = diag_ref[...]
    row = lax.broadcasted_iota(jnp.int32, (128, 128), 0)
    column = lax.broadcasted_iota(jnp.int32, (128, 128), 1)
    eye = jnp.where(row == column, 1.0, 0.0)
    m2 = jnp.dot(m1, m1, precision=HIGHEST)
    p1 = eye + m1 + m2 + jnp.dot(m1 + m2, m2, precision=HIGHEST)
    p2 = jnp.dot(p1, p1, precision=HIGHEST)
    p3 = jnp.dot(p2, p1, precision=HIGHEST)
    q2 = 0.75 * eye + 0.25 * p2
    q3 = (1.0 / 3.0) * eye + 0.5 * p1 + (1.0 / 6.0) * p3

    def stacked(matrix, m):
        rows = matrix[32 * m:32 * m + 32, :]
        for shift in (32, 64):
            rows = rows + pltpu.roll(rows, shift, 1)
        return stack_left(rows, 64)

    for m in range(4):
        pp_ref[32 * m:32 * m + 32, :] = stacked(p1, m)
        pp_ref[128 + 32 * m:128 + 32 * m + 32, :] = stacked(p2, m)

    idx = idx_ref[...]
    slot = lax.broadcasted_iota(jnp.int32, (1, SLOTS), 1)
    live = slot < count_ref[0, 0]
    frac = frac_ref[...]
    wpad_ref[...] = jnp.zeros((32, SLOTS), F32)
    sums = [0.0, 0.0, 0.0]
    for m in range(4):
        wpad_ref[0:27, :] = w_ref[:, m, :]
        left = jnp.concatenate([stacked(p1, m), stacked(q2, m), stacked(q3, m)], axis=0)
        values = dot(left, stack_right(wpad_ref[...]))
        for k in range(3):
            sums[k] = sums[k] + frac[m:m + 1, :] * values[32 * k:32 * k + 32]
        b3_ref[m] = values[64:96]
    first = jnp.where(live, sums[0], 0.0)
    first = jnp.concatenate([first[0:27], jnp.where(live, frac, 0.0), first[31:32]], axis=0)
    for k in range(2):
        c_ref[32 * k:32 * k + 32, :] = jnp.where(live, sums[k + 1], 0.0)

    hot = lane_hot(idx)
    for g in range(GROUPS):
        cols = slice(g * GROUP, (g + 1) * GROUP)
        dense = to_zones(stack_pair(first), hot, idx, g)
        u_ref[:, cols] = jnp.where(dense[27:28] > 0.0, dense, v_ref[:, cols])
        fm_ref[:, cols] = dense[24:32]


def stack_pair(x):
    return jnp.concatenate(halves(x), axis=0)


def to_zones(both, hot, idx, g):
    here = jnp.where(lax.shift_right_logical(idx, 8) == g, 1.0, 0.0).astype(BF16)
    dense = lax.dot_general(
        both * here, hot, (((1,), (1,)), ((), ())), preferred_element_type=F32
    )
    rows = both.shape[0] // 2
    return dense[0:rows] + dense[rows:]


def zones_kernel(after_ref, c_ref, idx_ref, c2_ref, c3_ref):
    idx = idx_ref[...]
    hot = lane_hot(idx)
    both = stack_pair(c_ref[...])
    for g in range(GROUPS):
        cols = slice(g * GROUP, (g + 1) * GROUP)
        dense = to_zones(both, hot, idx, g)
        c2_ref[:, cols] = dense[0:32]
        c3_ref[:, cols] = dense[32:64]


def inside(axis):
    at = lax.axis_index(axis)
    return at > 0, at < lax.axis_size(axis) - 1


def halo_x(xlo_ref, xhi_ref, pad_ref, first=0):
    for y in range(CY):
        pad_ref[0:9, block(y)] = xlo_ref[pl.ds(first + y, 9, stride=8), :]
        pad_ref[0:9, block(CY + y)] = xhi_ref[pl.ds(first + y, 9, stride=8), :]


def halo_y(ylo_ref, yhi_ref, pad_ref):
    low, high = inside("yz")
    for x in range(CX):
        pad_ref[0:9, block(16 + x)] = jnp.where(low, ylo_ref[pl.ds(x, 9, stride=4), :], 0.0)
        pad_ref[0:9, block(20 + x)] = jnp.where(high, yhi_ref[pl.ds(x, 9, stride=4), :], 0.0)


def terms(fh_ref, pad_ref, face):
    first, last = ((0, 1024), (1024, 2048), (2048, 2560), (2560, 3072))[face]
    return dot(fh_ref[32 * face:32 * face + 32, :], stack_right(pad_ref[:, first:last]))


def halo_add(int_ref, fh_ref, pad_ref, rate_ref, along_x, along_y):
    x_low, x_high = [terms(fh_ref, pad_ref, face) for face in (0, 1)] if along_x else (None, None)
    y_low, y_high = [terms(fh_ref, pad_ref, face) for face in (2, 3)] if along_y else (None, None)
    for x in range(CX):
        for y in range(CY):
            r = x * CY + y
            total = int_ref[:, block(r)]
            if along_x and x == 0:
                total += x_low[:, block(y)]
            if along_x and x == CX - 1:
                total += x_high[:, block(y)]
            if along_y and y == 0:
                total += y_low[:, block(x)]
            if along_y and y == CY - 1:
                total += y_high[:, block(x)]
            rate_ref[:, block(r)] = total


def x_faces(v_ref, xlo_ref, xhi_ref, first=0):
    for y in range(CY):
        xlo_ref[pl.ds(first + y, 9, stride=8), :] = v_ref[0:9, block(y)]
        xhi_ref[pl.ds(first + y, 9, stride=8), :] = v_ref[18:27, block(24 + y)]


def y_faces(v_ref, ylo_ref, yhi_ref):
    for x in range(CX):
        for a in range(3):
            ylo_ref[pl.ds(12 * a + x, 3, stride=4), :] = v_ref[9 * a:9 * a + 3, block(8 * x)]
            yhi_ref[pl.ds(12 * a + x, 3, stride=4), :] = v_ref[9 * a + 6:9 * a + 9, block(8 * x + 7)]


def y_first_kernel(
    int_ref, u_ref, v_ref, fh_ref, yl_ref, yh_ref, rate_ref, xlo_ref, xhi_ref, pad_ref,
):
    pad_ref[...] = jnp.zeros((16, 3072), F32)
    halo_y(yl_ref, yh_ref, pad_ref)
    halo_add(int_ref, fh_ref, pad_ref, rate_ref, False, True)
    x_faces(v_ref, xlo_ref, xhi_ref)
    for y in range(CY):
        xlo_ref[pl.ds(72 + y, 9, stride=8), :] = u_ref[0:9, block(y)] + rate_ref[0:9, block(y)]
        xhi_ref[pl.ds(72 + y, 9, stride=8), :] = (
            u_ref[18:27, block(24 + y)] + rate_ref[18:27, block(24 + y)]
        )


def x_first_kernel(
    int_ref, u_ref, v_ref, fh_ref, xl_ref, xh_ref,
    next_ref, rate_ref, beside_ref, ylo_ref, yhi_ref, pad_ref, own_ref,
):
    pad_ref[...] = jnp.zeros((16, 3072), F32)
    halo_x(xl_ref, xh_ref, pad_ref)
    halo_add(int_ref, fh_ref, pad_ref, rate_ref, True, False)
    next_ref[...] = u_ref[...] + rate_ref[...]
    y_faces(next_ref, ylo_ref, yhi_ref)
    own_ref[...] = jnp.zeros((16, 2048), F32)
    own_ref[0:9, 0:1024] = v_ref[0:9, 0:1024]
    own_ref[0:9, 1024:2048] = v_ref[18:27, 3072:4096]
    to_low = dot(fh_ref[32:64, :], stack_right(own_ref[:, 0:1024]))
    to_high = dot(fh_ref[0:32, :], stack_right(own_ref[:, 1024:2048]))
    low, high = inside("gx")
    halo_x(xl_ref, xh_ref, pad_ref, 72)
    beside_ref[...] = jnp.zeros((16, 2048), F32)
    beside_ref[0:9, 0:1024] = pad_ref[0:9, 0:1024] + jnp.where(low, to_low[18:27], 0.0)
    beside_ref[0:9, 1024:2048] = pad_ref[0:9, 1024:2048] + jnp.where(high, to_high[0:9], 0.0)


def second_kernel(
    int_ref, u_ref, fh_ref, yl_ref, yh_ref,
    v_ref, rate_ref, xlo_ref, xhi_ref, ylo_ref, yhi_ref, pad_ref,
):
    pad_ref[...] = jnp.zeros((16, 3072), F32)
    halo_y(yl_ref, yh_ref, pad_ref)
    halo_add(int_ref, fh_ref, pad_ref, rate_ref, False, True)
    v_ref[...] = u_ref[...] + 0.25 * rate_ref[...]
    x_faces(v_ref, xlo_ref, xhi_ref)
    y_faces(v_ref, ylo_ref, yhi_ref)


def between_one(
    v0_ref, v1_ref, r_ref, beside_ref, c2_ref, c3_ref, fm_ref, idx_ref, wg_ref, fh_ref, pp_ref, b3_ref,
    int_ref, u_ref, c3_out, b3_out, g_ref,
):
    interior(v1_ref, wg_ref, g_ref, int_ref)
    int_ref[:, 0:1024] += terms(fh_ref, beside_ref, 0)
    int_ref[:, 3072:4096] += terms(fh_ref, beside_ref, 1)
    for x in range(CX):
        cols = slice(x * 1024, (x + 1) * 1024)
        q = dot(pp_ref[...], stack_right(r_ref[:, cols]))
        f = fm_ref[:, cols]
        s1 = sum(f[m + 3:m + 4] * q[32 * m:32 * m + 32] for m in range(4))
        s2 = sum(f[m + 3:m + 4] * q[128 + 32 * m:160 + 32 * m] for m in range(4))
        bulk = 0.75 * v0_ref[:, cols] + 0.25 * v1_ref[:, cols]
        u_ref[:, cols] = jnp.where(f[3:4] > 0.0, c2_ref[:, cols] + 0.25 * s1, bulk)
        c3_out[:, cols] = c3_ref[:, cols] + (1.0 / 6.0) * s2
    idx = idx_ref[...]
    at = stack_right(to_slots(r_ref, lane_hot(idx), idx))
    for m in range(4):
        b3_out[m] = b3_ref[m] + (1.0 / 6.0) * dot(pp_ref[128 + 32 * m:160 + 32 * m, :], at)


def between_two(
    v0_ref, v2_ref, r_ref, c3_ref, fm_ref, idx_ref, wg_ref, pp_ref, b3_ref,
    int_ref, u_ref, b3_out, g_ref,
):
    interior(v2_ref, wg_ref, g_ref, int_ref)
    for x in range(CX):
        cols = slice(x * 1024, (x + 1) * 1024)
        q = dot(pp_ref[0:128, :], stack_right(r_ref[:, cols]))
        f = fm_ref[:, cols]
        s1 = sum(f[m + 3:m + 4] * q[32 * m:32 * m + 32] for m in range(4))
        bulk = (1.0 / 3.0) * v0_ref[:, cols] + (2.0 / 3.0) * v2_ref[:, cols]
        u_ref[:, cols] = jnp.where(f[3:4] > 0.0, c3_ref[:, cols] + (1.0 / 6.0) * s1, bulk)
    idx = idx_ref[...]
    at = stack_right(to_slots(r_ref, lane_hot(idx), idx))
    for m in range(4):
        b3_out[m] = b3_ref[m] + (1.0 / 6.0) * dot(pp_ref[32 * m:32 * m + 32, :], at)


def last_kernel(
    count_ref, int_ref, u_ref, fh_ref, xl_ref, xh_ref, yl_ref, yh_ref, idx_ref, b3_ref, w_ref,
    field_hbm, out_hbm, pad_ref, rate_ref, field_ref, out_ref, sems,
):
    pad_ref[...] = jnp.zeros((16, 3072), F32)
    halo_x(xl_ref, xh_ref, pad_ref)
    halo_y(yl_ref, yh_ref, pad_ref)
    halo_add(int_ref, fh_ref, pad_ref, rate_ref, True, True)
    for r in range(ROWS):
        value = u_ref[0:27, block(r)] + (2.0 / 3.0) * rate_ref[0:27, block(r)]
        field_ref[pl.ds(r, 27, stride=32), :] = value
    field_copy = pltpu.make_async_copy(field_ref, field_hbm, sems.at[0])
    field_copy.start()
    idx = idx_ref[...]
    at = (2.0 / 3.0) * to_slots(rate_ref, lane_hot(idx), idx)
    live = lax.broadcasted_iota(jnp.int32, (1, SLOTS), 1) < count_ref[0, 0]
    for m in range(4):
        out_ref[:, m, :] = jnp.where(live, b3_ref[m, 0:27, :] + at[0:27], w_ref[:, m, :])
    out_copy = pltpu.make_async_copy(out_ref, out_hbm, sems.at[1])
    out_copy.start()
    field_copy.wait()
    out_copy.wait()


VMEM = pl.BlockSpec(memory_space=pltpu.VMEM)
SMEM = pl.BlockSpec(memory_space=pltpu.SMEM)
ANY = pl.BlockSpec(memory_space=pl.ANY)
DENSE = jax.ShapeDtypeStruct((32, ZONES), F32)
X_FACES = [jax.ShapeDtypeStruct((72, 128), F32)] * 2
X_TWICE = [jax.ShapeDtypeStruct((144, 128), F32)] * 2
Y_FACES = [jax.ShapeDtypeStruct((36, 128), F32)] * 2
SLOT3 = jax.ShapeDtypeStruct((4, 32, SLOTS), F32)


def call(kernel, outs, args, scratch=(), smem=0, flops=0, in_spec=VMEM, out_spec=VMEM):
    specs = [SMEM] * smem + [in_spec] * (len(args) - smem)
    moved = 4 * sum(int(np.prod(a.shape)) for a in list(args) + list(outs))
    return pl.pallas_call(
        kernel,
        out_shape=outs,
        in_specs=specs,
        out_specs=[out_spec] * len(outs),
        scratch_shapes=list(scratch),
        compiler_params=pltpu.CompilerParams(vmem_limit_bytes=48 * 1024 * 1024),
        cost_estimate=pl.CostEstimate(flops=flops, bytes_accessed=moved, transcendentals=0),
    )(*args)


def exchange_x(low, high):
    n = lax.axis_size("gx")
    below = lax.ppermute(high, "gx", [(i, i + 1) for i in range(n - 1)])
    above = lax.ppermute(low, "gx", [(i + 1, i) for i in range(n - 1)])
    return below, above


def exchange_y(low, high):
    n = lax.axis_size("yz")
    below = lax.ppermute(high, "yz", [(i, (i + 1) % n) for i in range(n)])
    above = lax.ppermute(low, "yz", [(i, (i - 1) % n) for i in range(n)])
    return below, above


def on_device(
    state, mix_weights, mix_frac, mix_index, mix_count, vol_matrix, face_matrix, mat_matrix
):
    flat = state.reshape(27 * ROWS, CZ)
    small = [
        mix_weights.reshape(4, 27, SLOTS).transpose(1, 0, 2),
        mix_frac.reshape(4, SLOTS),
        mix_index.reshape(1, SLOTS),
        vol_matrix,
        face_matrix,
        mat_matrix.transpose(1, 0, 2),
        jnp.asarray(selections(), BF16),
    ]
    count = mix_count.reshape(1, 1)
    g_space = pltpu.VMEM((224, ZONES), F32)
    pad = pltpu.VMEM((16, 3072), F32)
    bf = lambda rows, lanes: jax.ShapeDtypeStruct((rows, lanes), BF16)
    f32 = lambda rows, lanes: jax.ShapeDtypeStruct((rows, lanes), F32)

    v0, *out = call(
        first_kernel,
        [DENSE] + Y_FACES + [jax.ShapeDtypeStruct(a.shape, a.dtype) for a in small],
        [flat] + small,
        [pltpu.VMEM((27 * ROWS, CZ), F32), pltpu.SemaphoreType.DMA((8,))],
        in_spec=ANY,
    )
    halo = exchange_y(*out[:2])
    small = out[2:]
    weights, idx = small[0], small[2]
    inner, u, fm, wg, fh, pp, b3, rest = call(
        mixed_kernel,
        [DENSE, DENSE, f32(8, ZONES), bf(224, 128), bf(128, 64), bf(256, 128), SLOT3, f32(64, SLOTS)],
        [count, v0] + small,
        [g_space, pltpu.VMEM((32, 128), F32), pltpu.VMEM((128, 128), F32),
         pltpu.VMEM((32, SLOTS), F32)],
        smem=1, flops=3 * 10**9,
    )
    inner, *faces = call(
        y_first_kernel, [DENSE] + X_TWICE, [inner, u, v0, fh, *halo], [pad]
    )
    halo = exchange_x(*faces)
    c2, c3 = call(zones_kernel, [DENSE, DENSE], [faces[0], rest, idx], flops=2 * 10**9)
    v1, r0, beside, *faces = call(
        x_first_kernel, [DENSE, DENSE, f32(16, 2048)] + Y_FACES, [inner, u, v0, fh, *halo],
        [pad, pltpu.VMEM((16, 2048), F32)],
    )
    halo = exchange_y(*faces)
    inner, u, c3, b3 = call(
        between_one, [DENSE, DENSE, DENSE, SLOT3],
        [v0, v1, r0, beside, c2, c3, fm, idx, wg, fh, pp, b3], [g_space], flops=2 * 10**9,
    )
    v2, r1, *faces = call(
        second_kernel, [DENSE, DENSE] + X_FACES + Y_FACES, [inner, u, fh, *halo], [pad]
    )
    y_halo = exchange_y(*faces[2:])
    x_halo = exchange_x(*faces[:2])
    inner, u, b3 = call(
        between_two, [DENSE, DENSE, SLOT3],
        [v0, v2, r1, c3, fm, idx, wg, pp, b3], [g_space], flops=2 * 10**9,
    )
    field, out = call(
        last_kernel,
        [jax.ShapeDtypeStruct((27 * ROWS, CZ), F32), jax.ShapeDtypeStruct((27, 4, SLOTS), F32)],
        [count, inner, u, fh, *x_halo, *y_halo, idx, b3, weights],
        [pad, pltpu.VMEM((32, ZONES), F32), pltpu.VMEM((27 * ROWS, CZ), F32),
         pltpu.VMEM((27, 4, SLOTS), F32), pltpu.SemaphoreType.DMA((2,))],
        smem=1, out_spec=ANY,
    )
    return field.reshape(state.shape), out.transpose(1, 0, 2).reshape(mix_weights.shape)


def solution(mesh):
    placed = (
        P(None, "gx", "yz", None),
        P("gx", "yz", None, None, None),
        P("gx", "yz", None, None),
        P("gx", "yz", None),
        P("gx", "yz"),
        P(),
        P(),
        P(),
    )
    return jax.shard_map(
        on_device,
        mesh=mesh,
        in_specs=placed,
        out_specs=(P(None, "gx", "yz", None), P("gx", "yz", None, None, None)),
        check_vma=False,
    )
```

```python
import numpy as np
import jax
import jax.numpy as jnp
from jax import lax
from jax.experimental import pallas as pl
from jax.experimental.pallas import tpu as pltpu
from jax.sharding import PartitionSpec as P

F32 = jnp.float32
BF16 = jnp.bfloat16
CX, CY, CZ = 4, 8, 128
ROWS = CX * CY
ZONES = ROWS * CZ
SLOTS = 1024
GROUP = 256
GROUPS = ZONES // GROUP


def face_dofs(face, own):
    axis, high = divmod(face, 2)
    at = (2 if high else 0) if own else (0 if high else 2)
    dofs = []
    for p in range(3):
        for q in range(3):
            abc = [p, q]
            abc.insert(axis, at)
            dofs.append(abc[0] * 9 + abc[1] * 3 + abc[2])
    return dofs


def selections():
    sel = np.zeros((64, 7 * 128 + 4 * 64), np.float32)
    for face in range(6):
        for q in range(9):
            row = 9 * face + q
            for copy in range(4):
                sel[row, copy * 32 + face_dofs(face, True)[q]] -= 1.0
                sel[row, (face + 1) * 128 + copy * 32 + face_dofs(face, False)[q]] += 1.0
                if face < 4:
                    sel[row, 7 * 128 + face * 64 + copy * 16 + q] += 1.0
    return sel


def halves(x):
    hi = x.astype(BF16)
    lo = (x - hi.astype(F32)).astype(BF16)
    return hi, lo


def stack_right(x):
    hi, lo = halves(x)
    return jnp.concatenate([hi, lo, hi, lo], axis=0)


def stack_left(x, half):
    hi = x.astype(BF16).astype(F32)
    lane = lax.broadcasted_iota(jnp.int32, x.shape, 1)
    return jnp.where(lane < half, hi, x - hi).astype(BF16)


def dot(a, b):
    return jnp.dot(a, b, preferred_element_type=F32)


def product(a, b):
    a_hi, a_lo = halves(a)
    b_hi, b_lo = halves(b)
    left = jnp.concatenate([a_hi, a_lo], axis=1)
    return dot(left, jnp.concatenate([b_hi, b_hi], axis=0)) + dot(a_hi, b_lo)


def block(r):
    return slice(r * CZ, (r + 1) * CZ)


def interior(v_ref, wg_ref, g_ref, out_ref):
    for x in range(CX):
        cols = slice(x * 1024, (x + 1) * 1024)
        g_ref[:, cols] = dot(wg_ref[...], stack_right(v_ref[:, cols]))
    lane = lax.broadcasted_iota(jnp.int32, (32, CZ), 1)
    for x in range(CX):
        for y in range(CY):
            r = x * CY + y
            total = g_ref[0:32, block(r)]
            if x > 0:
                total += g_ref[32:64, block(r - CY)]
            if x < CX - 1:
                total += g_ref[64:96, block(r + CY)]
            if y > 0:
                total += g_ref[96:128, block(r - 1)]
            if y < CY - 1:
                total += g_ref[128:160, block(r + 1)]
            below = pltpu.roll(g_ref[160:192, block(r)], 1, 1)
            above = pltpu.roll(g_ref[192:224, block(r)], CZ - 1, 1)
            total += jnp.where(lane == 0, 0.0, below)
            total += jnp.where(lane == CZ - 1, 0.0, above)
            out_ref[:, block(r)] = total


def lane_hot(idx):
    place = lax.broadcasted_iota(jnp.int32, (GROUP, SLOTS), 0)
    return jnp.where(place == (idx & (GROUP - 1)), 1.0, 0.0).astype(BF16)


def to_slots(r_ref, hot, idx):
    group = lax.shift_right_logical(idx, 8)
    parts = []
    for g in range(GROUPS):
        parts += halves(r_ref[:, g * GROUP:(g + 1) * GROUP])
    taken = dot(jnp.concatenate(parts, axis=0), hot)
    total = jnp.zeros((32, SLOTS), F32)
    for g in range(GROUPS):
        both = taken[64 * g:64 * g + 32] + taken[64 * g + 32:64 * g + 64]
        total = jnp.where(group == g, both, total)
    return total


def first_kernel(*refs):
    count = 8
    sources, (v_ref, ylo_ref, yhi_ref), rest = refs[:count], refs[count:count + 3], refs[count + 3:]
    targets, (state_ref, sems) = rest[:count - 1], rest[count - 1:]
    copies = [
        pltpu.make_async_copy(source, target, sems.at[k])
        for k, (source, target) in enumerate(zip(sources, (state_ref,) + targets))
    ]
    for copy in copies:
        copy.start()
    v_ref[24:32, :] = jnp.zeros((8, ZONES), F32)
    copies[0].wait()
    for q in range(9):
        low, high = face_dofs(2, True)[q], face_dofs(3, True)[q]
        ylo_ref[q * 4:q * 4 + 4, :] = state_ref[pl.ds(low * 32, 4, stride=8), :]
        yhi_ref[q * 4:q * 4 + 4, :] = state_ref[pl.ds(high * 32 + 7, 4, stride=8), :]
    for r in range(ROWS):
        v_ref[0:27, block(r)] = state_ref[pl.ds(r, 27, stride=32), :]
    for copy in copies[1:]:
        copy.wait()


def mixed_kernel(
    count_ref, v_ref, w_ref, frac_ref, idx_ref, vol_ref, face_ref, mat_ref, sel_ref,
    int_ref, u_ref, fm_ref, wg_ref, fh_ref, pp_ref, b3_ref, c_ref,
    g_ref, small_ref, diag_ref, wpad_ref,
):
    small_ref[...] = jnp.zeros((32, 128), F32)
    small_ref[0:27, 0:54] = face_ref[...]
    f_hi, f_lo = halves(small_ref[:, 0:64])
    sel = sel_ref[...].astype(BF16)
    laid = dot(f_hi, sel) + dot(f_lo, sel)
    small_ref[...] = jnp.zeros((32, 128), F32)
    small_ref[0:27, 0:27] = vol_ref[...]
    vol = small_ref[...]
    vol4 = vol + pltpu.roll(vol, 32, 1)
    vol4 = vol4 + pltpu.roll(vol4, 64, 1)
    wg_ref[0:32, :] = stack_left(laid[:, 0:128] + vol4, 64)
    for k in range(1, 7):
        wg_ref[32 * k:32 * k + 32, :] = stack_left(laid[:, 128 * k:128 * k + 128], 64)
    for k in range(4):
        first = 7 * 128 + 64 * k
        fh_ref[32 * k:32 * k + 32, :] = stack_left(laid[:, first:first + 64], 32)
    interior(v_ref, wg_ref, g_ref, int_ref)

    for m in range(4):
        small_ref[0:27, 0:27] = mat_ref[:, m, :]
        small = small_ref[...]
        diag_ref[32 * m:32 * m + 32, :] = pltpu.roll(small, 32 * m, 1) if m else small
    m1 = diag_ref[...]
    row = lax.broadcasted_iota(jnp.int32, (128, 128), 0)
    column = lax.broadcasted_iota(jnp.int32, (128, 128), 1)
    eye = jnp.where(row == column, 1.0, 0.0)
    m2 = product(m1, m1)
    p1 = eye + m1 + m2 + product(m1 + m2, m2)
    p2 = product(p1, p1)
    p3 = product(p2, p1)
    q2 = 0.75 * eye + 0.25 * p2
    q3 = (1.0 / 3.0) * eye + 0.5 * p1 + (1.0 / 6.0) * p3

    def stacked(matrix, m):
        rows = matrix[32 * m:32 * m + 32, :]
        for shift in (32, 64):
            rows = rows + pltpu.roll(rows, shift, 1)
        return stack_left(rows, 64)

    for m in range(4):
        pp_ref[32 * m:32 * m + 32, :] = stacked(p1, m)
        pp_ref[128 + 32 * m:128 + 32 * m + 32, :] = stacked(p2, m)

    idx = idx_ref[...]
    slot = lax.broadcasted_iota(jnp.int32, (1, SLOTS), 1)
    live = slot < count_ref[0, 0]
    frac = frac_ref[...]
    wpad_ref[...] = jnp.zeros((32, SLOTS), F32)
    sums = [0.0, 0.0, 0.0]
    for m in range(4):
        wpad_ref[0:27, :] = w_ref[:, m, :]
        left = jnp.concatenate([stacked(p1, m), stacked(q2, m), stacked(q3, m)], axis=0)
        values = dot(left, stack_right(wpad_ref[...]))
        for k in range(3):
            sums[k] = sums[k] + frac[m:m + 1, :] * values[32 * k:32 * k + 32]
        b3_ref[m] = values[64:96]
    first = jnp.where(live, sums[0], 0.0)
    first = jnp.concatenate([first[0:27], jnp.where(live, frac, 0.0), first[31:32]], axis=0)
    for k in range(2):
        c_ref[32 * k:32 * k + 32, :] = jnp.where(live, sums[k + 1], 0.0)

    hot = lane_hot(idx)
    dense = to_zones(first, hot, idx)
    for g in range(GROUPS):
        cols = slice(g * GROUP, (g + 1) * GROUP)
        here = dense[g]
        u_ref[:, cols] = jnp.where(here[27:28] > 0.0, here, v_ref[:, cols])
        fm_ref[:, cols] = here[24:32]


def to_zones(values, hot, idx):
    both = jnp.concatenate(halves(values), axis=0)
    group = lax.shift_right_logical(idx, 8)
    parts = [both * jnp.where(group == g, 1.0, 0.0).astype(BF16) for g in range(GROUPS)]
    dense = lax.dot_general(
        jnp.concatenate(parts, axis=0), hot, (((1,), (1,)), ((), ())), preferred_element_type=F32
    )
    rows = values.shape[0]
    return [
        dense[2 * rows * g:2 * rows * g + rows] + dense[2 * rows * g + rows:2 * rows * (g + 1)]
        for g in range(GROUPS)
    ]


def zones_kernel(after_ref, c_ref, idx_ref, c2_ref, c3_ref):
    idx = idx_ref[...]
    dense = to_zones(c_ref[...], lane_hot(idx), idx)
    for g in range(GROUPS):
        cols = slice(g * GROUP, (g + 1) * GROUP)
        c2_ref[:, cols] = dense[g][0:32]
        c3_ref[:, cols] = dense[g][32:64]


def inside(axis):
    at = lax.axis_index(axis)
    return at > 0, at < lax.axis_size(axis) - 1


def halo_x(xlo_ref, xhi_ref, pad_ref, first=0):
    for y in range(CY):
        pad_ref[0:9, block(y)] = xlo_ref[pl.ds(first + y, 9, stride=8), :]
        pad_ref[0:9, block(CY + y)] = xhi_ref[pl.ds(first + y, 9, stride=8), :]


def halo_y(ylo_ref, yhi_ref, pad_ref):
    low, high = inside("yz")
    for x in range(CX):
        pad_ref[0:9, block(16 + x)] = jnp.where(low, ylo_ref[pl.ds(x, 9, stride=4), :], 0.0)
        pad_ref[0:9, block(20 + x)] = jnp.where(high, yhi_ref[pl.ds(x, 9, stride=4), :], 0.0)


def terms(fh_ref, pad_ref, face):
    first, last = ((0, 1024), (1024, 2048), (2048, 2560), (2560, 3072))[face]
    return dot(fh_ref[32 * face:32 * face + 32, :], stack_right(pad_ref[:, first:last]))


def halo_add(int_ref, fh_ref, pad_ref, rate_ref, along_x, along_y):
    x_low, x_high = [terms(fh_ref, pad_ref, face) for face in (0, 1)] if along_x else (None, None)
    y_low, y_high = [terms(fh_ref, pad_ref, face) for face in (2, 3)] if along_y else (None, None)
    for x in range(CX):
        for y in range(CY):
            r = x * CY + y
            total = int_ref[:, block(r)]
            if along_x and x == 0:
                total += x_low[:, block(y)]
            if along_x and x == CX - 1:
                total += x_high[:, block(y)]
            if along_y and y == 0:
                total += y_low[:, block(x)]
            if along_y and y == CY - 1:
                total += y_high[:, block(x)]
            rate_ref[:, block(r)] = total


def x_faces(v_ref, xlo_ref, xhi_ref, first=0):
    for y in range(CY):
        xlo_ref[pl.ds(first + y, 9, stride=8), :] = v_ref[0:9, block(y)]
        xhi_ref[pl.ds(first + y, 9, stride=8), :] = v_ref[18:27, block(24 + y)]


def y_faces(v_ref, ylo_ref, yhi_ref):
    for x in range(CX):
        for a in range(3):
            ylo_ref[pl.ds(12 * a + x, 3, stride=4), :] = v_ref[9 * a:9 * a + 3, block(8 * x)]
            yhi_ref[pl.ds(12 * a + x, 3, stride=4), :] = v_ref[9 * a + 6:9 * a + 9, block(8 * x + 7)]


def y_first_kernel(
    int_ref, u_ref, v_ref, fh_ref, yl_ref, yh_ref, rate_ref, xlo_ref, xhi_ref, pad_ref,
):
    pad_ref[...] = jnp.zeros((16, 3072), F32)
    halo_y(yl_ref, yh_ref, pad_ref)
    halo_add(int_ref, fh_ref, pad_ref, rate_ref, False, True)
    x_faces(v_ref, xlo_ref, xhi_ref)
    for y in range(CY):
        xlo_ref[pl.ds(72 + y, 9, stride=8), :] = u_ref[0:9, block(y)] + rate_ref[0:9, block(y)]
        xhi_ref[pl.ds(72 + y, 9, stride=8), :] = (
            u_ref[18:27, block(24 + y)] + rate_ref[18:27, block(24 + y)]
        )


def x_first_kernel(
    int_ref, u_ref, v_ref, fh_ref, xl_ref, xh_ref,
    next_ref, rate_ref, beside_ref, ylo_ref, yhi_ref, pad_ref, own_ref,
):
    pad_ref[...] = jnp.zeros((16, 3072), F32)
    halo_x(xl_ref, xh_ref, pad_ref)
    halo_add(int_ref, fh_ref, pad_ref, rate_ref, True, False)
    next_ref[...] = u_ref[...] + rate_ref[...]
    y_faces(next_ref, ylo_ref, yhi_ref)
    own_ref[...] = jnp.zeros((16, 2048), F32)
    own_ref[0:9, 0:1024] = v_ref[0:9, 0:1024]
    own_ref[0:9, 1024:2048] = v_ref[18:27, 3072:4096]
    to_low = dot(fh_ref[32:64, :], stack_right(own_ref[:, 0:1024]))
    to_high = dot(fh_ref[0:32, :], stack_right(own_ref[:, 1024:2048]))
    low, high = inside("gx")
    halo_x(xl_ref, xh_ref, pad_ref, 72)
    beside_ref[...] = jnp.zeros((16, 2048), F32)
    beside_ref[0:9, 0:1024] = pad_ref[0:9, 0:1024] + jnp.where(low, to_low[18:27], 0.0)
    beside_ref[0:9, 1024:2048] = pad_ref[0:9, 1024:2048] + jnp.where(high, to_high[0:9], 0.0)


def second_kernel(
    int_ref, u_ref, fh_ref, yl_ref, yh_ref,
    v_ref, rate_ref, xlo_ref, xhi_ref, ylo_ref, yhi_ref, pad_ref,
):
    pad_ref[...] = jnp.zeros((16, 3072), F32)
    halo_y(yl_ref, yh_ref, pad_ref)
    halo_add(int_ref, fh_ref, pad_ref, rate_ref, False, True)
    v_ref[...] = u_ref[...] + 0.25 * rate_ref[...]
    x_faces(v_ref, xlo_ref, xhi_ref)
    y_faces(v_ref, ylo_ref, yhi_ref)


def between_one(
    v0_ref, v1_ref, r_ref, beside_ref, c2_ref, c3_ref, fm_ref, idx_ref, wg_ref, fh_ref, pp_ref, b3_ref,
    int_ref, u_ref, c3_out, b3_out, g_ref,
):
    interior(v1_ref, wg_ref, g_ref, int_ref)
    int_ref[:, 0:1024] += terms(fh_ref, beside_ref, 0)
    int_ref[:, 3072:4096] += terms(fh_ref, beside_ref, 1)
    for x in range(CX):
        cols = slice(x * 1024, (x + 1) * 1024)
        q = dot(pp_ref[...], stack_right(r_ref[:, cols]))
        f = fm_ref[:, cols]
        s1 = sum(f[m + 3:m + 4] * q[32 * m:32 * m + 32] for m in range(4))
        s2 = sum(f[m + 3:m + 4] * q[128 + 32 * m:160 + 32 * m] for m in range(4))
        bulk = 0.75 * v0_ref[:, cols] + 0.25 * v1_ref[:, cols]
        u_ref[:, cols] = jnp.where(f[3:4] > 0.0, c2_ref[:, cols] + 0.25 * s1, bulk)
        c3_out[:, cols] = c3_ref[:, cols] + (1.0 / 6.0) * s2
    idx = idx_ref[...]
    at = stack_right(to_slots(r_ref, lane_hot(idx), idx))
    for m in range(4):
        b3_out[m] = b3_ref[m] + (1.0 / 6.0) * dot(pp_ref[128 + 32 * m:160 + 32 * m, :], at)


def between_two(
    v0_ref, v2_ref, r_ref, c3_ref, fm_ref, idx_ref, wg_ref, pp_ref, b3_ref,
    int_ref, u_ref, b3_out, g_ref,
):
    interior(v2_ref, wg_ref, g_ref, int_ref)
    for x in range(CX):
        cols = slice(x * 1024, (x + 1) * 1024)
        q = dot(pp_ref[0:128, :], stack_right(r_ref[:, cols]))
        f = fm_ref[:, cols]
        s1 = sum(f[m + 3:m + 4] * q[32 * m:32 * m + 32] for m in range(4))
        bulk = (1.0 / 3.0) * v0_ref[:, cols] + (2.0 / 3.0) * v2_ref[:, cols]
        u_ref[:, cols] = jnp.where(f[3:4] > 0.0, c3_ref[:, cols] + (1.0 / 6.0) * s1, bulk)
    idx = idx_ref[...]
    at = stack_right(to_slots(r_ref, lane_hot(idx), idx))
    for m in range(4):
        b3_out[m] = b3_ref[m] + (1.0 / 6.0) * dot(pp_ref[32 * m:32 * m + 32, :], at)


def last_kernel(
    count_ref, int_ref, u_ref, fh_ref, xl_ref, xh_ref, yl_ref, yh_ref, idx_ref, b3_ref, w_ref,
    field_hbm, out_hbm, pad_ref, rate_ref, field_ref, out_ref, sems,
):
    pad_ref[...] = jnp.zeros((16, 3072), F32)
    halo_x(xl_ref, xh_ref, pad_ref)
    halo_y(yl_ref, yh_ref, pad_ref)
    halo_add(int_ref, fh_ref, pad_ref, rate_ref, True, True)
    for r in range(ROWS):
        value = u_ref[0:27, block(r)] + (2.0 / 3.0) * rate_ref[0:27, block(r)]
        field_ref[pl.ds(r, 27, stride=32), :] = value
    field_copy = pltpu.make_async_copy(field_ref, field_hbm, sems.at[0])
    field_copy.start()
    idx = idx_ref[...]
    at = (2.0 / 3.0) * to_slots(rate_ref, lane_hot(idx), idx)
    live = lax.broadcasted_iota(jnp.int32, (1, SLOTS), 1) < count_ref[0, 0]
    for m in range(4):
        out_ref[:, m, :] = jnp.where(live, b3_ref[m, 0:27, :] + at[0:27], w_ref[:, m, :])
    out_copy = pltpu.make_async_copy(out_ref, out_hbm, sems.at[1])
    out_copy.start()
    field_copy.wait()
    out_copy.wait()


VMEM = pl.BlockSpec(memory_space=pltpu.VMEM)
SMEM = pl.BlockSpec(memory_space=pltpu.SMEM)
ANY = pl.BlockSpec(memory_space=pl.ANY)
HBM = pl.BlockSpec(memory_space=pltpu.HBM)
DENSE = jax.ShapeDtypeStruct((32, ZONES), F32)
X_FACES = [jax.ShapeDtypeStruct((72, 128), F32)] * 2
X_TWICE = [jax.ShapeDtypeStruct((144, 128), F32)] * 2
Y_FACES = [jax.ShapeDtypeStruct((36, 128), F32)] * 2
SLOT3 = jax.ShapeDtypeStruct((4, 32, SLOTS), F32)


def call(kernel, outs, args, scratch=(), smem=0, flops=0, in_spec=VMEM, out_spec=VMEM, vmem=48):
    specs = [SMEM] * smem + [in_spec] * (len(args) - smem)
    moved = 4 * sum(int(np.prod(a.shape)) for a in list(args) + list(outs))
    return pl.pallas_call(
        kernel,
        out_shape=outs,
        in_specs=specs,
        out_specs=[out_spec] * len(outs),
        scratch_shapes=list(scratch),
        compiler_params=pltpu.CompilerParams(vmem_limit_bytes=vmem * 1024 * 1024),
        cost_estimate=pl.CostEstimate(flops=flops, bytes_accessed=moved, transcendentals=0),
    )(*args)


def exchange_x(low, high):
    n = lax.axis_size("gx")
    below = lax.ppermute(high, "gx", [(i, i + 1) for i in range(n - 1)])
    above = lax.ppermute(low, "gx", [(i + 1, i) for i in range(n - 1)])
    return below, above


def exchange_y(low, high):
    n = lax.axis_size("yz")
    below = lax.ppermute(high, "yz", [(i, (i + 1) % n) for i in range(n)])
    above = lax.ppermute(low, "yz", [(i, (i - 1) % n) for i in range(n)])
    return below, above


def on_device(
    state, mix_weights, mix_frac, mix_index, mix_count, vol_matrix, face_matrix, mat_matrix
):
    flat = state.reshape(27 * ROWS, CZ)
    small = [
        mix_weights.reshape(4, 27, SLOTS).transpose(1, 0, 2),
        mix_frac.reshape(4, SLOTS),
        mix_index.reshape(1, SLOTS),
        vol_matrix,
        face_matrix,
        mat_matrix.transpose(1, 0, 2),
        jnp.asarray(selections()),
    ]
    count = mix_count.reshape(1, 1)
    g_space = pltpu.VMEM((224, ZONES), F32)
    pad = pltpu.VMEM((16, 3072), F32)
    bf = lambda rows, lanes: jax.ShapeDtypeStruct((rows, lanes), BF16)
    f32 = lambda rows, lanes: jax.ShapeDtypeStruct((rows, lanes), F32)

    v0, *out = call(
        first_kernel,
        [DENSE] + Y_FACES + [jax.ShapeDtypeStruct(a.shape, a.dtype) for a in small],
        [pltpu.with_memory_space_constraint(a, pltpu.HBM) for a in [flat] + small],
        [pltpu.VMEM((27 * ROWS, CZ), F32), pltpu.SemaphoreType.DMA((8,))],
        in_spec=HBM,
    )
    halo = exchange_y(*out[:2])
    small = out[2:]
    weights, idx = small[0], small[2]
    inner, u, fm, wg, fh, pp, b3, rest = call(
        mixed_kernel,
        [DENSE, DENSE, f32(8, ZONES), bf(224, 128), bf(128, 64), bf(256, 128), SLOT3, f32(64, SLOTS)],
        [count, v0] + small,
        [g_space, pltpu.VMEM((32, 128), F32), pltpu.VMEM((128, 128), F32),
         pltpu.VMEM((32, SLOTS), F32)],
        smem=1, flops=3 * 10**9,
    )
    inner, *faces = call(
        y_first_kernel, [DENSE] + X_TWICE, [inner, u, v0, fh, *halo], [pad]
    )
    halo = exchange_x(*faces)
    c2, c3 = call(zones_kernel, [DENSE, DENSE], [faces[0], rest, idx], flops=2 * 10**9)
    v1, r0, beside, *faces = call(
        x_first_kernel, [DENSE, DENSE, f32(16, 2048)] + Y_FACES, [inner, u, v0, fh, *halo],
        [pad, pltpu.VMEM((16, 2048), F32)],
    )
    halo = exchange_y(*faces)
    inner, u, c3, b3 = call(
        between_one, [DENSE, DENSE, DENSE, SLOT3],
        [v0, v1, r0, beside, c2, c3, fm, idx, wg, fh, pp, b3], [g_space], flops=2 * 10**9,
    )
    v2, r1, *faces = call(
        second_kernel, [DENSE, DENSE] + X_FACES + Y_FACES, [inner, u, fh, *halo], [pad]
    )
    y_halo = exchange_y(*faces[2:])
    x_halo = exchange_x(*faces[:2])
    inner, u, b3 = call(
        between_two, [DENSE, DENSE, SLOT3],
        [v0, v2, r1, c3, fm, idx, wg, pp, b3], [g_space], flops=2 * 10**9,
    )
    field, out = call(
        last_kernel,
        [jax.ShapeDtypeStruct((27 * ROWS, CZ), F32), jax.ShapeDtypeStruct((27, 4, SLOTS), F32)],
        [count, inner, u, fh, *x_halo, *y_halo, idx, b3, weights],
        [pad, pltpu.VMEM((32, ZONES), F32), pltpu.VMEM((27 * ROWS, CZ), F32),
         pltpu.VMEM((27, 4, SLOTS), F32), pltpu.SemaphoreType.DMA((2,))],
        smem=1, out_spec=ANY,
    )
    return field.reshape(state.shape), out.transpose(1, 0, 2).reshape(mix_weights.shape)


def solution(mesh):
    placed = (
        P(None, "gx", "yz", None),
        P("gx", "yz", None, None, None),
        P("gx", "yz", None, None),
        P("gx", "yz", None),
        P("gx", "yz"),
        P(),
        P(),
        P(),
    )
    return jax.shard_map(
        on_device,
        mesh=mesh,
        in_specs=placed,
        out_specs=(P(None, "gx", "yz", None), P("gx", "yz", None, None, None)),
        check_vma=False,
    )
```

```python
import numpy as np
import jax
import jax.numpy as jnp
from jax import lax
from jax.experimental import pallas as pl
from jax.experimental.pallas import tpu as pltpu
from jax.sharding import PartitionSpec as P

F32 = jnp.float32
BF16 = jnp.bfloat16
CX, CY, CZ = 4, 8, 128
ROWS = CX * CY
ZONES = ROWS * CZ
SLOTS = 1024
GROUP = 256
GROUPS = ZONES // GROUP


def face_dofs(face, own):
    axis, high = divmod(face, 2)
    at = (2 if high else 0) if own else (0 if high else 2)
    dofs = []
    for p in range(3):
        for q in range(3):
            abc = [p, q]
            abc.insert(axis, at)
            dofs.append(abc[0] * 9 + abc[1] * 3 + abc[2])
    return dofs


def selections():
    sel = np.zeros((64, 7 * 128 + 2 * 256), np.float32)
    for face in range(6):
        for q in range(9):
            row = 9 * face + q
            for copy in range(4):
                sel[row, copy * 32 + face_dofs(face, True)[q]] -= 1.0
                sel[row, (face + 1) * 128 + copy * 32 + face_dofs(face, False)[q]] += 1.0
                if face < 4:
                    sel[row, 7 * 128 + face * 64 + copy * 16 + q] += 1.0
                    sel[row, 9 * 128 + copy * 64 + face * 16 + q] += 1.0
    return sel


def halves(x):
    hi = x.astype(BF16)
    lo = (x - hi.astype(F32)).astype(BF16)
    return hi, lo


def stack_right(x):
    hi, lo = halves(x)
    return jnp.concatenate([hi, lo, hi, lo], axis=0)


def stack_left(x, half):
    hi = x.astype(BF16).astype(F32)
    lane = lax.broadcasted_iota(jnp.int32, x.shape, 1)
    return jnp.where(lane < half, hi, x - hi).astype(BF16)


def dot(a, b):
    return jnp.dot(a, b, preferred_element_type=F32)


def product(a, b):
    a_hi, a_lo = halves(a)
    b_hi, b_lo = halves(b)
    left = jnp.concatenate([a_hi, a_lo], axis=1)
    return dot(left, jnp.concatenate([b_hi, b_hi], axis=0)) + dot(a_hi, b_lo)


def block(r):
    return slice(r * CZ, (r + 1) * CZ)


def interior(v_ref, wg_ref, g_ref, out_ref):
    for x in range(CX):
        cols = slice(x * 1024, (x + 1) * 1024)
        g_ref[:, cols] = dot(wg_ref[...], stack_right(v_ref[:, cols]))
    lane = lax.broadcasted_iota(jnp.int32, (32, CZ), 1)
    for x in range(CX):
        for y in range(CY):
            r = x * CY + y
            total = g_ref[0:32, block(r)]
            if x > 0:
                total += g_ref[32:64, block(r - CY)]
            if x < CX - 1:
                total += g_ref[64:96, block(r + CY)]
            if y > 0:
                total += g_ref[96:128, block(r - 1)]
            if y < CY - 1:
                total += g_ref[128:160, block(r + 1)]
            below = pltpu.roll(g_ref[160:192, block(r)], 1, 1)
            above = pltpu.roll(g_ref[192:224, block(r)], CZ - 1, 1)
            total += jnp.where(lane == 0, 0.0, below)
            total += jnp.where(lane == CZ - 1, 0.0, above)
            out_ref[:, block(r)] = total


def lane_hot(idx):
    place = lax.broadcasted_iota(jnp.int32, (GROUP, SLOTS), 0)
    return jnp.where(place == (idx & (GROUP - 1)), 1.0, 0.0).astype(BF16)


def to_slots(r_ref, hot, idx):
    group = lax.shift_right_logical(idx, 8)
    parts = []
    for g in range(GROUPS):
        parts += halves(r_ref[:, g * GROUP:(g + 1) * GROUP])
    taken = dot(jnp.concatenate(parts, axis=0), hot)
    total = jnp.zeros((32, SLOTS), F32)
    for g in range(GROUPS):
        both = taken[64 * g:64 * g + 32] + taken[64 * g + 32:64 * g + 64]
        total = jnp.where(group == g, both, total)
    return total


def first_kernel(*refs):
    count = 8
    sources, (v_ref, ylo_ref, yhi_ref), rest = refs[:count], refs[count:count + 3], refs[count + 3:]
    targets, (state_ref, sems) = rest[:count - 1], rest[count - 1:]
    copies = [
        pltpu.make_async_copy(source, target, sems.at[k])
        for k, (source, target) in enumerate(zip(sources, (state_ref,) + targets))
    ]
    for copy in copies:
        copy.start()
    v_ref[24:32, :] = jnp.zeros((8, ZONES), F32)
    copies[0].wait()
    for q in range(9):
        low, high = face_dofs(2, True)[q], face_dofs(3, True)[q]
        ylo_ref[q * 4:q * 4 + 4, :] = state_ref[pl.ds(low * 32, 4, stride=8), :]
        yhi_ref[q * 4:q * 4 + 4, :] = state_ref[pl.ds(high * 32 + 7, 4, stride=8), :]
    for r in range(ROWS):
        v_ref[0:27, block(r)] = state_ref[pl.ds(r, 27, stride=32), :]
    for copy in copies[1:]:
        copy.wait()


def mixed_kernel(
    count_ref, v_ref, w_ref, frac_ref, idx_ref, vol_ref, face_ref, mat_ref, sel_ref,
    int_ref, u_ref, fm_ref, wg_ref, fh_ref, fs_ref, power_ref,
    g_ref, small_ref, diag_ref, wpad_ref,
):
    small_ref[...] = jnp.zeros((32, 128), F32)
    small_ref[0:27, 0:54] = face_ref[...]
    f_hi, f_lo = halves(small_ref[:, 0:64])
    sel = sel_ref[...].astype(BF16)
    laid = dot(f_hi, sel) + dot(f_lo, sel)
    small_ref[...] = jnp.zeros((32, 128), F32)
    small_ref[0:27, 0:27] = vol_ref[...]
    vol = small_ref[...]
    vol4 = vol + pltpu.roll(vol, 32, 1)
    vol4 = vol4 + pltpu.roll(vol4, 64, 1)
    wg_ref[0:32, :] = stack_left(laid[:, 0:128] + vol4, 64)
    for k in range(1, 7):
        wg_ref[32 * k:32 * k + 32, :] = stack_left(laid[:, 128 * k:128 * k + 128], 64)
    for k in range(4):
        first = 7 * 128 + 64 * k
        fh_ref[32 * k:32 * k + 32, :] = stack_left(laid[:, first:first + 64], 32)
    fs_ref[...] = stack_left(laid[:, 9 * 128:11 * 128], 128)
    interior(v_ref, wg_ref, g_ref, int_ref)

    for m in range(4):
        small_ref[0:27, 0:27] = mat_ref[:, m, :]
        small = small_ref[...]
        diag_ref[32 * m:32 * m + 32, :] = pltpu.roll(small, 32 * m, 1) if m else small
    m1 = diag_ref[...]
    m2 = product(m1, m1)
    p1 = identity() + m1 + m2 + product(m1 + m2, m2)
    power_ref[...] = p1

    idx = idx_ref[...]
    frac = frac_ref[...]
    wpad_ref[...] = jnp.zeros((32, SLOTS), F32)
    first = 0.0
    for m in range(4):
        wpad_ref[0:27, :] = w_ref[:, m, :]
        values = dot(stacked(p1, m), stack_right(wpad_ref[...]))
        first = first + frac[m:m + 1, :] * values
    live = slots_live(count_ref)
    first = jnp.where(live, first, 0.0)
    first = jnp.concatenate([first[0:27], jnp.where(live, frac, 0.0), first[31:32]], axis=0)

    dense = to_zones(first, lane_hot(idx), idx)
    for g in range(GROUPS):
        cols = slice(g * GROUP, (g + 1) * GROUP)
        here = dense[g]
        u_ref[:, cols] = jnp.where(here[27:28] > 0.0, here, v_ref[:, cols])
        fm_ref[:, cols] = here[24:32]


def identity():
    row = lax.broadcasted_iota(jnp.int32, (128, 128), 0)
    column = lax.broadcasted_iota(jnp.int32, (128, 128), 1)
    return jnp.where(row == column, 1.0, 0.0)


def slots_live(count_ref):
    return lax.broadcasted_iota(jnp.int32, (1, SLOTS), 1) < count_ref[0, 0]


def stacked(matrix, m):
    rows = matrix[32 * m:32 * m + 32, :]
    for shift in (32, 64):
        rows = rows + pltpu.roll(rows, shift, 1)
    return stack_left(rows, 64)


def to_zones(values, hot, idx):
    both = jnp.concatenate(halves(values), axis=0)
    group = lax.shift_right_logical(idx, 8)
    parts = [both * jnp.where(group == g, 1.0, 0.0).astype(BF16) for g in range(GROUPS)]
    dense = lax.dot_general(
        jnp.concatenate(parts, axis=0), hot, (((1,), (1,)), ((), ())), preferred_element_type=F32
    )
    rows = values.shape[0]
    return [
        dense[2 * rows * g:2 * rows * g + rows] + dense[2 * rows * g + rows:2 * rows * (g + 1)]
        for g in range(GROUPS)
    ]


def later_kernel(
    count_ref, after_ref, power_ref, w_ref, frac_ref, idx_ref,
    c2_ref, c3_ref, pp_ref, b3_ref, wpad_ref,
):
    eye = identity()
    p1 = power_ref[...]
    p2 = product(p1, p1)
    q2 = 0.75 * eye + 0.25 * p2
    q3 = (1.0 / 3.0) * eye + 0.5 * p1 + (1.0 / 6.0) * product(p2, p1)
    frac = frac_ref[...]
    wpad_ref[...] = jnp.zeros((32, SLOTS), F32)
    total = 0.0
    for m in range(4):
        pp_ref[32 * m:32 * m + 32, :] = stacked(p1, m)
        pp_ref[128 + 32 * m:160 + 32 * m, :] = stacked(p2, m)
        wpad_ref[0:27, :] = w_ref[:, m, :]
        left = jnp.concatenate([stacked(q2, m), stacked(q3, m)], axis=0)
        values = dot(left, stack_right(wpad_ref[...]))
        b3_ref[m] = values[32:64]
        total = total + frac[m:m + 1, :] * values
    idx = idx_ref[...]
    dense = to_zones(jnp.where(slots_live(count_ref), total, 0.0), lane_hot(idx), idx)
    for g in range(GROUPS):
        cols = slice(g * GROUP, (g + 1) * GROUP)
        c2_ref[:, cols] = dense[g][0:32]
        c3_ref[:, cols] = dense[g][32:64]


def inside(axis):
    at = lax.axis_index(axis)
    return at > 0, at < lax.axis_size(axis) - 1


def halo_x(xlo_ref, xhi_ref, pad_ref, first=0):
    for y in range(CY):
        pad_ref[0:9, block(y)] = xlo_ref[pl.ds(first + y, 9, stride=8), :]
        pad_ref[0:9, block(CY + y)] = xhi_ref[pl.ds(first + y, 9, stride=8), :]


def halo_y(ylo_ref, yhi_ref, pad_ref):
    low, high = inside("yz")
    for x in range(CX):
        pad_ref[0:9, block(16 + x)] = jnp.where(low, ylo_ref[pl.ds(x, 9, stride=4), :], 0.0)
        pad_ref[0:9, block(20 + x)] = jnp.where(high, yhi_ref[pl.ds(x, 9, stride=4), :], 0.0)


def terms(fh_ref, pad_ref, face):
    first, last = ((0, 1024), (1024, 2048), (2048, 2560), (2560, 3072))[face]
    return dot(fh_ref[32 * face:32 * face + 32, :], stack_right(pad_ref[:, first:last]))


def halo_add(int_ref, fh_ref, pad_ref, rate_ref, along_x, along_y):
    x_low, x_high = [terms(fh_ref, pad_ref, face) for face in (0, 1)] if along_x else (None, None)
    y_low, y_high = [terms(fh_ref, pad_ref, face) for face in (2, 3)] if along_y else (None, None)
    for x in range(CX):
        for y in range(CY):
            r = x * CY + y
            total = int_ref[:, block(r)]
            if along_x and x == 0:
                total += x_low[:, block(y)]
            if along_x and x == CX - 1:
                total += x_high[:, block(y)]
            if along_y and y == 0:
                total += y_low[:, block(x)]
            if along_y and y == CY - 1:
                total += y_high[:, block(x)]
            rate_ref[:, block(r)] = total


def x_faces(v_ref, xlo_ref, xhi_ref, first=0):
    for y in range(CY):
        xlo_ref[pl.ds(first + y, 9, stride=8), :] = v_ref[0:9, block(y)]
        xhi_ref[pl.ds(first + y, 9, stride=8), :] = v_ref[18:27, block(24 + y)]


def y_faces(v_ref, ylo_ref, yhi_ref):
    for x in range(CX):
        for a in range(3):
            ylo_ref[pl.ds(12 * a + x, 3, stride=4), :] = v_ref[9 * a:9 * a + 3, block(8 * x)]
            yhi_ref[pl.ds(12 * a + x, 3, stride=4), :] = v_ref[9 * a + 6:9 * a + 9, block(8 * x + 7)]


def y_first_kernel(
    int_ref, u_ref, v_ref, fh_ref, yl_ref, yh_ref, rate_ref, xlo_ref, xhi_ref, pad_ref,
):
    pad_ref[...] = jnp.zeros((16, 3072), F32)
    halo_y(yl_ref, yh_ref, pad_ref)
    halo_add(int_ref, fh_ref, pad_ref, rate_ref, False, True)
    x_faces(v_ref, xlo_ref, xhi_ref)
    for y in range(CY):
        xlo_ref[pl.ds(72 + y, 9, stride=8), :] = u_ref[0:9, block(y)] + rate_ref[0:9, block(y)]
        xhi_ref[pl.ds(72 + y, 9, stride=8), :] = (
            u_ref[18:27, block(24 + y)] + rate_ref[18:27, block(24 + y)]
        )


def x_first_kernel(
    int_ref, u_ref, v_ref, fh_ref, xl_ref, xh_ref,
    next_ref, rate_ref, beside_ref, ylo_ref, yhi_ref, pad_ref, own_ref,
):
    pad_ref[...] = jnp.zeros((16, 3072), F32)
    halo_x(xl_ref, xh_ref, pad_ref)
    halo_add(int_ref, fh_ref, pad_ref, rate_ref, True, False)
    next_ref[...] = u_ref[...] + rate_ref[...]
    y_faces(next_ref, ylo_ref, yhi_ref)
    own_ref[...] = jnp.zeros((16, 2048), F32)
    own_ref[0:9, 0:1024] = v_ref[0:9, 0:1024]
    own_ref[0:9, 1024:2048] = v_ref[18:27, 3072:4096]
    to_low = dot(fh_ref[32:64, :], stack_right(own_ref[:, 0:1024]))
    to_high = dot(fh_ref[0:32, :], stack_right(own_ref[:, 1024:2048]))
    low, high = inside("gx")
    halo_x(xl_ref, xh_ref, pad_ref, 72)
    beside_ref[...] = jnp.zeros((16, 2048), F32)
    beside_ref[0:9, 0:1024] = pad_ref[0:9, 0:1024] + jnp.where(low, to_low[18:27], 0.0)
    beside_ref[0:9, 1024:2048] = pad_ref[0:9, 1024:2048] + jnp.where(high, to_high[0:9], 0.0)


def second_kernel(
    int_ref, u_ref, fh_ref, yl_ref, yh_ref,
    v_ref, rate_ref, xlo_ref, xhi_ref, ylo_ref, yhi_ref, pad_ref,
):
    pad_ref[...] = jnp.zeros((16, 3072), F32)
    halo_y(yl_ref, yh_ref, pad_ref)
    halo_add(int_ref, fh_ref, pad_ref, rate_ref, False, True)
    v_ref[...] = u_ref[...] + 0.25 * rate_ref[...]
    x_faces(v_ref, xlo_ref, xhi_ref)
    y_faces(v_ref, ylo_ref, yhi_ref)


def between_one(
    v0_ref, v1_ref, r_ref, beside_ref, c2_ref, c3_ref, fm_ref, idx_ref, wg_ref, fh_ref, pp_ref, b3_ref,
    int_ref, u_ref, c3_out, b3_out, g_ref,
):
    interior(v1_ref, wg_ref, g_ref, int_ref)
    int_ref[:, 0:1024] += terms(fh_ref, beside_ref, 0)
    int_ref[:, 3072:4096] += terms(fh_ref, beside_ref, 1)
    for x in range(CX):
        cols = slice(x * 1024, (x + 1) * 1024)
        q = dot(pp_ref[...], stack_right(r_ref[:, cols]))
        f = fm_ref[:, cols]
        s1 = sum(f[m + 3:m + 4] * q[32 * m:32 * m + 32] for m in range(4))
        s2 = sum(f[m + 3:m + 4] * q[128 + 32 * m:160 + 32 * m] for m in range(4))
        bulk = 0.75 * v0_ref[:, cols] + 0.25 * v1_ref[:, cols]
        u_ref[:, cols] = jnp.where(f[3:4] > 0.0, c2_ref[:, cols] + 0.25 * s1, bulk)
        c3_out[:, cols] = c3_ref[:, cols] + (1.0 / 6.0) * s2
    idx = idx_ref[...]
    at = stack_right(to_slots(r_ref, lane_hot(idx), idx))
    for m in range(4):
        b3_out[m] = b3_ref[m] + (1.0 / 6.0) * dot(pp_ref[128 + 32 * m:160 + 32 * m, :], at)


def between_two(
    v0_ref, v2_ref, r_ref, c3_ref, fm_ref, idx_ref, wg_ref, pp_ref, b3_ref,
    u_ref, b3_out, g_ref, int_ref,
):
    interior(v2_ref, wg_ref, g_ref, int_ref)
    for x in range(CX):
        cols = slice(x * 1024, (x + 1) * 1024)
        q = dot(pp_ref[0:128, :], stack_right(r_ref[:, cols]))
        f = fm_ref[:, cols]
        s1 = sum(f[m + 3:m + 4] * q[32 * m:32 * m + 32] for m in range(4))
        bulk = (1.0 / 3.0) * v0_ref[:, cols] + (2.0 / 3.0) * v2_ref[:, cols]
        old = jnp.where(f[3:4] > 0.0, c3_ref[:, cols] + (1.0 / 6.0) * s1, bulk)
        u_ref[:, cols] = old + (2.0 / 3.0) * int_ref[:, cols]
    idx = idx_ref[...]
    hot = lane_hot(idx)
    at = stack_right(to_slots(r_ref, hot, idx))
    inner = (2.0 / 3.0) * to_slots(int_ref, hot, idx)
    for m in range(4):
        b3_out[m] = b3_ref[m] + inner + (1.0 / 6.0) * dot(pp_ref[32 * m:32 * m + 32, :], at)


def faces_to_slots(pad_ref, idx):
    parts = []
    for g in range(8):
        parts += halves(pad_ref[:, g * GROUP:(g + 1) * GROUP])
    for x in range(CX):
        low, high = pad_ref[:, block(16 + x)], pad_ref[:, block(20 + x)]
        parts += halves(jnp.concatenate([low, high], axis=1))
    taken = dot(jnp.concatenate(parts, axis=0), lane_hot(idx))
    taken = [taken[32 * k:32 * k + 16] + taken[32 * k + 16:32 * k + 32] for k in range(12)]
    group = lax.shift_right_logical(idx, 8)
    x, y = lax.shift_right_logical(idx, 10), lax.shift_right_logical(idx, 7) & 7
    x_low = x_high = beside = jnp.zeros((16, SLOTS), F32)
    for k in range(4):
        x_low = jnp.where(group == k, taken[k], x_low)
        x_high = jnp.where(group == 12 + k, taken[4 + k], x_high)
        beside = jnp.where(x == k, taken[8 + k], beside)
    y_low, y_high = jnp.where(y == 0, beside, 0.0), jnp.where(y == CY - 1, beside, 0.0)
    return jnp.concatenate([x_low, x_high, y_low, y_high], axis=0)


def last_kernel(
    count_ref, u_ref, fh_ref, fs_ref, yl_ref, yh_ref, xl_ref, xh_ref, idx_ref, b3_ref, w_ref,
    field_hbm, out_hbm, pad_ref, whole_ref, field_ref, out_ref, sems,
):
    pad_ref[...] = jnp.zeros((16, 3072), F32)
    halo_x(xl_ref, xh_ref, pad_ref)
    halo_y(yl_ref, yh_ref, pad_ref)
    pad_ref[...] = (2.0 / 3.0) * pad_ref[...]
    halo_add(u_ref, fh_ref, pad_ref, whole_ref, True, True)
    for r in range(ROWS):
        field_ref[pl.ds(r, 27, stride=32), :] = whole_ref[0:27, block(r)]
    field_copy = pltpu.make_async_copy(field_ref, field_hbm, sems.at[0])
    field_copy.start()
    added = dot(fs_ref[...], stack_right(faces_to_slots(pad_ref, idx_ref[...])))
    live = slots_live(count_ref)
    for m in range(4):
        out_ref[:, m, :] = jnp.where(live, b3_ref[m, 0:27, :] + added[0:27], w_ref[:, m, :])
    out_copy = pltpu.make_async_copy(out_ref, out_hbm, sems.at[1])
    out_copy.start()
    field_copy.wait()
    out_copy.wait()


VMEM = pl.BlockSpec(memory_space=pltpu.VMEM)
SMEM = pl.BlockSpec(memory_space=pltpu.SMEM)
ANY = pl.BlockSpec(memory_space=pl.ANY)
HBM = pl.BlockSpec(memory_space=pltpu.HBM)
DENSE = jax.ShapeDtypeStruct((32, ZONES), F32)
X_FACES = [jax.ShapeDtypeStruct((72, 128), F32)] * 2
X_TWICE = [jax.ShapeDtypeStruct((144, 128), F32)] * 2
Y_FACES = [jax.ShapeDtypeStruct((36, 128), F32)] * 2
SLOT3 = jax.ShapeDtypeStruct((4, 32, SLOTS), F32)


def call(kernel, outs, args, scratch=(), smem=0, flops=0, in_spec=VMEM, out_spec=VMEM):
    moved = 4 * sum(int(np.prod(a.shape)) for a in list(args) + list(outs))
    return pl.pallas_call(
        kernel,
        out_shape=outs,
        in_specs=[SMEM] * smem + [in_spec] * (len(args) - smem),
        out_specs=[out_spec] * len(outs),
        scratch_shapes=list(scratch),
        compiler_params=pltpu.CompilerParams(vmem_limit_bytes=48 * 1024 * 1024),
        cost_estimate=pl.CostEstimate(flops=flops, bytes_accessed=moved, transcendentals=0),
    )(*args)


def exchange_x(low, high):
    n = lax.axis_size("gx")
    below = lax.ppermute(high, "gx", [(i, i + 1) for i in range(n - 1)])
    above = lax.ppermute(low, "gx", [(i + 1, i) for i in range(n - 1)])
    return below, above


def exchange_y(low, high):
    n = lax.axis_size("yz")
    below = lax.ppermute(high, "yz", [(i, (i + 1) % n) for i in range(n)])
    above = lax.ppermute(low, "yz", [(i, (i - 1) % n) for i in range(n)])
    return below, above


def on_device(
    state, mix_weights, mix_frac, mix_index, mix_count, vol_matrix, face_matrix, mat_matrix
):
    flat = state.reshape(27 * ROWS, CZ)
    small = [
        mix_weights.reshape(4, 27, SLOTS).transpose(1, 0, 2),
        mix_frac.reshape(4, SLOTS),
        mix_index.reshape(1, SLOTS),
        vol_matrix,
        face_matrix,
        mat_matrix.transpose(1, 0, 2),
        jnp.asarray(selections()),
    ]
    count = mix_count.reshape(1, 1)
    g_space = pltpu.VMEM((224, ZONES), F32)
    pad = pltpu.VMEM((16, 3072), F32)
    bf = lambda rows, lanes: jax.ShapeDtypeStruct((rows, lanes), BF16)
    f32 = lambda rows, lanes: jax.ShapeDtypeStruct((rows, lanes), F32)

    v0, *out = call(
        first_kernel,
        [DENSE] + Y_FACES + [jax.ShapeDtypeStruct(a.shape, a.dtype) for a in small],
        [pltpu.with_memory_space_constraint(a, pltpu.HBM) for a in [flat] + small],
        [pltpu.VMEM((27 * ROWS, CZ), F32), pltpu.SemaphoreType.DMA((8,))],
        in_spec=HBM,
    )
    halo = exchange_y(*out[:2])
    weights, frac, idx, *_ = small = out[2:]
    inner, u, fm, wg, fh, fs, power = call(
        mixed_kernel,
        [DENSE, DENSE, f32(8, ZONES), bf(224, 128), bf(128, 64), bf(32, 256), f32(128, 128)],
        [count, v0] + small,
        [g_space, pltpu.VMEM((32, 128), F32), pltpu.VMEM((128, 128), F32),
         pltpu.VMEM((32, SLOTS), F32)],
        smem=1, flops=3 * 10**9,
    )
    inner, *faces = call(
        y_first_kernel, [DENSE] + X_TWICE, [inner, u, v0, fh, *halo], [pad]
    )
    halo = exchange_x(*faces)
    c2, c3, pp, b3 = call(
        later_kernel, [DENSE, DENSE, bf(256, 128), SLOT3],
        [count, faces[0], power, weights, frac, idx], [pltpu.VMEM((32, SLOTS), F32)],
        smem=1, flops=2 * 10**9,
    )
    v1, r0, beside, *faces = call(
        x_first_kernel, [DENSE, DENSE, f32(16, 2048)] + Y_FACES, [inner, u, v0, fh, *halo],
        [pad, pltpu.VMEM((16, 2048), F32)],
    )
    halo = exchange_y(*faces)
    inner, u, c3, b3 = call(
        between_one, [DENSE, DENSE, DENSE, SLOT3],
        [v0, v1, r0, beside, c2, c3, fm, idx, wg, fh, pp, b3], [g_space], flops=2 * 10**9,
    )
    v2, r1, *faces = call(
        second_kernel, [DENSE, DENSE] + X_FACES + Y_FACES, [inner, u, fh, *halo], [pad]
    )
    x_halo = exchange_x(*faces[:2])
    y_halo = exchange_y(*faces[2:])
    u, b3 = call(
        between_two, [DENSE, SLOT3],
        [v0, v2, r1, c3, fm, idx, wg, pp, b3], [g_space, pltpu.VMEM((32, ZONES), F32)],
        flops=2 * 10**9,
    )
    field, out = call(
        last_kernel,
        [jax.ShapeDtypeStruct((27 * ROWS, CZ), F32), jax.ShapeDtypeStruct((27, 4, SLOTS), F32)],
        [count, u, fh, fs, *y_halo, *x_halo, idx, b3, weights],
        [pad, pltpu.VMEM((32, ZONES), F32), pltpu.VMEM((27 * ROWS, CZ), F32),
         pltpu.VMEM((27, 4, SLOTS), F32), pltpu.SemaphoreType.DMA((2,))],
        smem=1, out_spec=ANY,
    )
    return field.reshape(state.shape), out.transpose(1, 0, 2).reshape(mix_weights.shape)


def solution(mesh):
    placed = (
        P(None, "gx", "yz", None),
        P("gx", "yz", None, None, None),
        P("gx", "yz", None, None),
        P("gx", "yz", None),
        P("gx", "yz"),
        P(),
        P(),
        P(),
    )
    return jax.shard_map(
        on_device,
        mesh=mesh,
        in_specs=placed,
        out_specs=(P(None, "gx", "yz", None), P("gx", "yz", None, None, None)),
        check_vma=False,
    )
```

```python
import numpy as np
import jax
import jax.numpy as jnp
from jax import lax
from jax.experimental import pallas as pl
from jax.experimental.pallas import tpu as pltpu
from jax.sharding import PartitionSpec as P

F32 = jnp.float32
BF16 = jnp.bfloat16
CX, CY, CZ = 4, 8, 128
ROWS = CX * CY
ZONES = ROWS * CZ
SLOTS = 1024
GROUP = 256
GROUPS = ZONES // GROUP


def face_dofs(face, own):
    axis, high = divmod(face, 2)
    at = (2 if high else 0) if own else (0 if high else 2)
    dofs = []
    for p in range(3):
        for q in range(3):
            abc = [p, q]
            abc.insert(axis, at)
            dofs.append(abc[0] * 9 + abc[1] * 3 + abc[2])
    return dofs


def selections():
    sel = np.zeros((64, 7 * 128 + 2 * 256), np.float32)
    for face in range(6):
        for q in range(9):
            row = 9 * face + q
            for copy in range(4):
                sel[row, copy * 32 + face_dofs(face, True)[q]] -= 1.0
                sel[row, (face + 1) * 128 + copy * 32 + face_dofs(face, False)[q]] += 1.0
                if face < 4:
                    sel[row, 7 * 128 + face * 64 + copy * 16 + q] += 1.0
                    sel[row, 9 * 128 + copy * 64 + face * 16 + q] += 1.0
    return sel


def halves(x):
    hi = x.astype(BF16)
    lo = (x - hi.astype(F32)).astype(BF16)
    return hi, lo


def stack_right(x):
    hi, lo = halves(x)
    return jnp.concatenate([hi, lo, hi, lo], axis=0)


def stack_left(x, half):
    hi = x.astype(BF16).astype(F32)
    lane = lax.broadcasted_iota(jnp.int32, x.shape, 1)
    return jnp.where(lane < half, hi, x - hi).astype(BF16)


def dot(a, b):
    return jnp.dot(a, b, preferred_element_type=F32)


def product(a, b):
    a_hi, a_lo = halves(a)
    b_hi, b_lo = halves(b)
    left = jnp.concatenate([a_hi, a_lo], axis=1)
    return dot(left, jnp.concatenate([b_hi, b_hi], axis=0)) + dot(a_hi, b_lo)


def block(r):
    return slice(r * CZ, (r + 1) * CZ)


def interior(v_ref, wg_ref, g_ref, out_ref):
    for x in range(CX):
        cols = slice(x * 1024, (x + 1) * 1024)
        g_ref[:, cols] = dot(wg_ref[...], stack_right(v_ref[:, cols]))
    lane = lax.broadcasted_iota(jnp.int32, (32, CZ), 1)
    for x in range(CX):
        for y in range(CY):
            r = x * CY + y
            total = g_ref[0:32, block(r)]
            if x > 0:
                total += g_ref[32:64, block(r - CY)]
            if x < CX - 1:
                total += g_ref[64:96, block(r + CY)]
            if y > 0:
                total += g_ref[96:128, block(r - 1)]
            if y < CY - 1:
                total += g_ref[128:160, block(r + 1)]
            below = pltpu.roll(g_ref[160:192, block(r)], 1, 1)
            above = pltpu.roll(g_ref[192:224, block(r)], CZ - 1, 1)
            total += jnp.where(lane == 0, 0.0, below)
            total += jnp.where(lane == CZ - 1, 0.0, above)
            out_ref[:, block(r)] = total


def lane_hot(idx):
    place = lax.broadcasted_iota(jnp.int32, (GROUP, SLOTS), 0)
    return jnp.where(place == (idx & (GROUP - 1)), 1.0, 0.0).astype(BF16)


def to_slots(r_ref, hot, idx):
    group = lax.shift_right_logical(idx, 8)
    parts = []
    for g in range(GROUPS):
        parts += halves(r_ref[:, g * GROUP:(g + 1) * GROUP])
    taken = dot(jnp.concatenate(parts, axis=0), hot)
    total = jnp.zeros((32, SLOTS), F32)
    for g in range(GROUPS):
        both = taken[64 * g:64 * g + 32] + taken[64 * g + 32:64 * g + 64]
        total = jnp.where(group == g, both, total)
    return total


def first_kernel(*refs):
    count = 8
    sources, (v_ref, ylo_ref, yhi_ref), rest = refs[:count], refs[count:count + 3], refs[count + 3:]
    targets, (state_ref, sems) = rest[:count - 1], rest[count - 1:]
    copies = [
        pltpu.make_async_copy(source, target, sems.at[k])
        for k, (source, target) in enumerate(zip(sources, (state_ref,) + targets))
    ]
    for copy in copies:
        copy.start()
    v_ref[24:32, :] = jnp.zeros((8, ZONES), F32)
    copies[0].wait()
    for q in range(9):
        low, high = face_dofs(2, True)[q], face_dofs(3, True)[q]
        ylo_ref[q * 4:q * 4 + 4, :] = state_ref[pl.ds(low * 32, 4, stride=8), :]
        yhi_ref[q * 4:q * 4 + 4, :] = state_ref[pl.ds(high * 32 + 7, 4, stride=8), :]
    for r in range(ROWS):
        v_ref[0:27, block(r)] = state_ref[pl.ds(r, 27, stride=32), :]
    for copy in copies[1:]:
        copy.wait()


def mixed_kernel(
    live_ref, v_ref, w_ref, frac_ref, idx_ref, vol_ref, face_ref, mat_ref, sel_ref,
    int_ref, u_ref, fm_ref, wg_ref, fh_ref, fs_ref, power_ref,
    g_ref, small_ref, diag_ref, wpad_ref,
):
    small_ref[...] = jnp.zeros((32, 128), F32)
    small_ref[0:27, 0:54] = face_ref[...]
    f_hi, f_lo = halves(small_ref[:, 0:64])
    sel = sel_ref[...].astype(BF16)
    laid = dot(f_hi, sel) + dot(f_lo, sel)
    small_ref[...] = jnp.zeros((32, 128), F32)
    small_ref[0:27, 0:27] = vol_ref[...]
    vol = small_ref[...]
    vol4 = vol + pltpu.roll(vol, 32, 1)
    vol4 = vol4 + pltpu.roll(vol4, 64, 1)
    wg_ref[0:32, :] = stack_left(laid[:, 0:128] + vol4, 64)
    for k in range(1, 7):
        wg_ref[32 * k:32 * k + 32, :] = stack_left(laid[:, 128 * k:128 * k + 128], 64)
    for k in range(4):
        first = 7 * 128 + 64 * k
        fh_ref[32 * k:32 * k + 32, :] = stack_left(laid[:, first:first + 64], 32)
    fs_ref[...] = stack_left(laid[:, 9 * 128:11 * 128], 128)
    interior(v_ref, wg_ref, g_ref, int_ref)

    for m in range(4):
        small_ref[0:27, 0:27] = mat_ref[:, m, :]
        small = small_ref[...]
        diag_ref[32 * m:32 * m + 32, :] = pltpu.roll(small, 32 * m, 1) if m else small
    m1 = diag_ref[...]
    m2 = product(m1, m1)
    p1 = identity() + m1 + m2 + product(m1 + m2, m2)
    power_ref[...] = p1

    idx = idx_ref[...]
    frac = frac_ref[...]
    wpad_ref[...] = jnp.zeros((32, SLOTS), F32)
    first = 0.0
    for m in range(4):
        wpad_ref[0:27, :] = w_ref[:, m, :]
        values = dot(stacked(p1, m), stack_right(wpad_ref[...]))
        first = first + frac[m:m + 1, :] * values
    live = live_ref[...] > 0.0
    first = jnp.where(live, first, 0.0)
    first = jnp.concatenate([first[0:27], jnp.where(live, frac, 0.0), first[31:32]], axis=0)

    dense = to_zones(first, lane_hot(idx), idx)
    for g in range(GROUPS):
        cols = slice(g * GROUP, (g + 1) * GROUP)
        here = dense[g]
        u_ref[:, cols] = jnp.where(here[27:28] > 0.0, here, v_ref[:, cols])
        fm_ref[:, cols] = here[24:32]


def identity():
    row = lax.broadcasted_iota(jnp.int32, (128, 128), 0)
    column = lax.broadcasted_iota(jnp.int32, (128, 128), 1)
    return jnp.where(row == column, 1.0, 0.0)


def stacked(matrix, m):
    rows = matrix[32 * m:32 * m + 32, :]
    for shift in (32, 64):
        rows = rows + pltpu.roll(rows, shift, 1)
    return stack_left(rows, 64)


def to_zones(values, hot, idx):
    both = jnp.concatenate(halves(values), axis=0)
    group = lax.shift_right_logical(idx, 8)
    parts = [both * jnp.where(group == g, 1.0, 0.0).astype(BF16) for g in range(GROUPS)]
    dense = lax.dot_general(
        jnp.concatenate(parts, axis=0), hot, (((1,), (1,)), ((), ())), preferred_element_type=F32
    )
    rows = values.shape[0]
    return [
        dense[2 * rows * g:2 * rows * g + rows] + dense[2 * rows * g + rows:2 * rows * (g + 1)]
        for g in range(GROUPS)
    ]


def later_kernel(
    live_ref, after_ref, power_ref, w_ref, frac_ref, idx_ref,
    c2_ref, c3_ref, pp_ref, b3_ref, wpad_ref,
):
    eye = identity()
    p1 = power_ref[...]
    p2 = product(p1, p1)
    q2 = 0.75 * eye + 0.25 * p2
    q3 = (1.0 / 3.0) * eye + 0.5 * p1 + (1.0 / 6.0) * product(p2, p1)
    frac = frac_ref[...]
    wpad_ref[...] = jnp.zeros((32, SLOTS), F32)
    total = 0.0
    for m in range(4):
        pp_ref[32 * m:32 * m + 32, 0:128] = stacked(p1, m)
        pp_ref[32 * m:32 * m + 32, 128:256] = stacked(p2, m)
        wpad_ref[0:27, :] = w_ref[:, m, :]
        left = jnp.concatenate([stacked(q2, m), stacked(q3, m)], axis=0)
        values = dot(left, stack_right(wpad_ref[...]))
        b3_ref[m] = values[32:64]
        total = total + frac[m:m + 1, :] * values
    idx = idx_ref[...]
    dense = to_zones(jnp.where(live_ref[...] > 0.0, total, 0.0), lane_hot(idx), idx)
    for g in range(GROUPS):
        cols = slice(g * GROUP, (g + 1) * GROUP)
        c2_ref[:, cols] = dense[g][0:32]
        c3_ref[:, cols] = dense[g][32:64]


def inside(axis):
    at = lax.axis_index(axis)
    return at > 0, at < lax.axis_size(axis) - 1


def halo_x(xlo_ref, xhi_ref, pad_ref, first=0):
    for y in range(CY):
        pad_ref[0:9, block(y)] = xlo_ref[pl.ds(first + y, 9, stride=8), :]
        pad_ref[0:9, block(CY + y)] = xhi_ref[pl.ds(first + y, 9, stride=8), :]


def halo_y(ylo_ref, yhi_ref, pad_ref):
    low, high = inside("yz")
    for x in range(CX):
        pad_ref[0:9, block(16 + x)] = jnp.where(low, ylo_ref[pl.ds(x, 9, stride=4), :], 0.0)
        pad_ref[0:9, block(20 + x)] = jnp.where(high, yhi_ref[pl.ds(x, 9, stride=4), :], 0.0)


def terms(fh_ref, pad_ref, face):
    first, last = ((0, 1024), (1024, 2048), (2048, 2560), (2560, 3072))[face]
    return dot(fh_ref[32 * face:32 * face + 32, :], stack_right(pad_ref[:, first:last]))


def halo_add(int_ref, fh_ref, pad_ref, rate_ref, along_x, along_y):
    x_low, x_high = [terms(fh_ref, pad_ref, face) for face in (0, 1)] if along_x else (None, None)
    y_low, y_high = [terms(fh_ref, pad_ref, face) for face in (2, 3)] if along_y else (None, None)
    for x in range(CX):
        for y in range(CY):
            r = x * CY + y
            total = int_ref[:, block(r)]
            if along_x and x == 0:
                total += x_low[:, block(y)]
            if along_x and x == CX - 1:
                total += x_high[:, block(y)]
            if along_y and y == 0:
                total += y_low[:, block(x)]
            if along_y and y == CY - 1:
                total += y_high[:, block(x)]
            rate_ref[:, block(r)] = total


def x_faces(v_ref, xlo_ref, xhi_ref, first=0):
    for y in range(CY):
        xlo_ref[pl.ds(first + y, 9, stride=8), :] = v_ref[0:9, block(y)]
        xhi_ref[pl.ds(first + y, 9, stride=8), :] = v_ref[18:27, block(24 + y)]


def y_faces(v_ref, ylo_ref, yhi_ref):
    for x in range(CX):
        for a in range(3):
            ylo_ref[pl.ds(12 * a + x, 3, stride=4), :] = v_ref[9 * a:9 * a + 3, block(8 * x)]
            yhi_ref[pl.ds(12 * a + x, 3, stride=4), :] = v_ref[9 * a + 6:9 * a + 9, block(8 * x + 7)]


def y_first_kernel(
    int_ref, u_ref, v_ref, fh_ref, yl_ref, yh_ref, rate_ref, xlo_ref, xhi_ref, pad_ref,
):
    pad_ref[...] = jnp.zeros((16, 3072), F32)
    halo_y(yl_ref, yh_ref, pad_ref)
    halo_add(int_ref, fh_ref, pad_ref, rate_ref, False, True)
    x_faces(v_ref, xlo_ref, xhi_ref)
    for y in range(CY):
        xlo_ref[pl.ds(72 + y, 9, stride=8), :] = u_ref[0:9, block(y)] + rate_ref[0:9, block(y)]
        xhi_ref[pl.ds(72 + y, 9, stride=8), :] = (
            u_ref[18:27, block(24 + y)] + rate_ref[18:27, block(24 + y)]
        )


def x_first_kernel(
    int_ref, u_ref, v_ref, fh_ref, xl_ref, xh_ref,
    next_ref, rate_ref, beside_ref, ylo_ref, yhi_ref, pad_ref, own_ref,
):
    pad_ref[...] = jnp.zeros((16, 3072), F32)
    halo_x(xl_ref, xh_ref, pad_ref)
    halo_add(int_ref, fh_ref, pad_ref, rate_ref, True, False)
    next_ref[...] = u_ref[...] + rate_ref[...]
    y_faces(next_ref, ylo_ref, yhi_ref)
    own_ref[...] = jnp.zeros((16, 2048), F32)
    own_ref[0:9, 0:1024] = v_ref[0:9, 0:1024]
    own_ref[0:9, 1024:2048] = v_ref[18:27, 3072:4096]
    to_low = dot(fh_ref[32:64, :], stack_right(own_ref[:, 0:1024]))
    to_high = dot(fh_ref[0:32, :], stack_right(own_ref[:, 1024:2048]))
    low, high = inside("gx")
    halo_x(xl_ref, xh_ref, pad_ref, 72)
    beside_ref[...] = jnp.zeros((16, 2048), F32)
    beside_ref[0:9, 0:1024] = pad_ref[0:9, 0:1024] + jnp.where(low, to_low[18:27], 0.0)
    beside_ref[0:9, 1024:2048] = pad_ref[0:9, 1024:2048] + jnp.where(high, to_high[0:9], 0.0)


def second_kernel(
    int_ref, u_ref, fh_ref, yl_ref, yh_ref,
    v_ref, rate_ref, xlo_ref, xhi_ref, ylo_ref, yhi_ref, pad_ref,
):
    pad_ref[...] = jnp.zeros((16, 3072), F32)
    halo_y(yl_ref, yh_ref, pad_ref)
    halo_add(int_ref, fh_ref, pad_ref, rate_ref, False, True)
    v_ref[...] = u_ref[...] + 0.25 * rate_ref[...]
    x_faces(v_ref, xlo_ref, xhi_ref)
    y_faces(v_ref, ylo_ref, yhi_ref)


def weighted(f, q):
    return sum(f[m + 3:m + 4] * q[32 * m:32 * m + 32] for m in range(4))


def between_one(
    v0_ref, v1_ref, r_ref, beside_ref, c2_ref, fm_ref, wg_ref, fh_ref, pp_ref,
    int_ref, u_ref, g_ref,
):
    interior(v1_ref, wg_ref, g_ref, int_ref)
    int_ref[:, 0:1024] += terms(fh_ref, beside_ref, 0)
    int_ref[:, 3072:4096] += terms(fh_ref, beside_ref, 1)
    for x in range(CX):
        cols = slice(x * 1024, (x + 1) * 1024)
        f = fm_ref[:, cols]
        s1 = weighted(f, dot(pp_ref[:, 0:128], stack_right(r_ref[:, cols])))
        bulk = 0.75 * v0_ref[:, cols] + 0.25 * v1_ref[:, cols]
        u_ref[:, cols] = jnp.where(f[3:4] > 0.0, c2_ref[:, cols] + 0.25 * s1, bulk)


def between_two(
    v0_ref, v2_ref, r0_ref, r1_ref, c3_ref, fm_ref, live_ref, idx_ref, wg_ref, pp_ref, b3_ref, w_ref,
    u_ref, slots_ref, g_ref, int_ref,
):
    interior(v2_ref, wg_ref, g_ref, int_ref)
    for x in range(CX):
        cols = slice(x * 1024, (x + 1) * 1024)
        both = jnp.concatenate([stack_right(r1_ref[:, cols]), stack_right(r0_ref[:, cols])], axis=0)
        f = fm_ref[:, cols]
        s1 = weighted(f, dot(pp_ref[...], both))
        bulk = (1.0 / 3.0) * v0_ref[:, cols] + (2.0 / 3.0) * v2_ref[:, cols]
        old = jnp.where(f[3:4] > 0.0, c3_ref[:, cols] + (1.0 / 6.0) * s1, bulk)
        u_ref[:, cols] = old + (2.0 / 3.0) * int_ref[:, cols]
    idx = idx_ref[...]
    hot = lane_hot(idx)
    both = jnp.concatenate(
        [stack_right(to_slots(r1_ref, hot, idx)), stack_right(to_slots(r0_ref, hot, idx))], axis=0
    )
    inner = (2.0 / 3.0) * to_slots(int_ref, hot, idx)
    live = live_ref[...] > 0.0
    for m in range(4):
        value = b3_ref[m] + inner + (1.0 / 6.0) * dot(pp_ref[32 * m:32 * m + 32, :], both)
        slots_ref[:, m, :] = jnp.where(live, value[0:27], w_ref[:, m, :])


def faces_to_slots(pad_ref, idx):
    parts = []
    for g in range(8):
        parts += halves(pad_ref[:, g * GROUP:(g + 1) * GROUP])
    for x in range(CX):
        low, high = pad_ref[:, block(16 + x)], pad_ref[:, block(20 + x)]
        parts += halves(jnp.concatenate([low, high], axis=1))
    taken = dot(jnp.concatenate(parts, axis=0), lane_hot(idx))
    taken = [taken[32 * k:32 * k + 16] + taken[32 * k + 16:32 * k + 32] for k in range(12)]
    group = lax.shift_right_logical(idx, 8)
    x, y = lax.shift_right_logical(idx, 10), lax.shift_right_logical(idx, 7) & 7
    x_low = x_high = beside = jnp.zeros((16, SLOTS), F32)
    for k in range(4):
        x_low = jnp.where(group == k, taken[k], x_low)
        x_high = jnp.where(group == 12 + k, taken[4 + k], x_high)
        beside = jnp.where(x == k, taken[8 + k], beside)
    y_low, y_high = jnp.where(y == 0, beside, 0.0), jnp.where(y == CY - 1, beside, 0.0)
    return jnp.concatenate([x_low, x_high, y_low, y_high], axis=0)


def last_kernel(
    live_ref, u_ref, fh_ref, fs_ref, yl_ref, yh_ref, xl_ref, xh_ref, idx_ref, slots_ref,
    field_hbm, out_hbm, pad_ref, whole_ref, field_ref, out_ref, sems,
):
    pad_ref[...] = jnp.zeros((16, 3072), F32)
    halo_x(xl_ref, xh_ref, pad_ref)
    halo_y(yl_ref, yh_ref, pad_ref)
    pad_ref[...] = (2.0 / 3.0) * pad_ref[...]
    halo_add(u_ref, fh_ref, pad_ref, whole_ref, True, True)
    for r in range(ROWS):
        field_ref[pl.ds(r, 27, stride=32), :] = whole_ref[0:27, block(r)]
    field_copy = pltpu.make_async_copy(field_ref, field_hbm, sems.at[0])
    field_copy.start()
    added = dot(fs_ref[...], stack_right(faces_to_slots(pad_ref, idx_ref[...])))
    added = jnp.where(live_ref[...] > 0.0, added, 0.0)
    for d in range(27):
        out_ref[d] = slots_ref[d] + added[d:d + 1]
    out_copy = pltpu.make_async_copy(out_ref, out_hbm, sems.at[1])
    out_copy.start()
    field_copy.wait()
    out_copy.wait()


VMEM = pl.BlockSpec(memory_space=pltpu.VMEM)
ANY = pl.BlockSpec(memory_space=pl.ANY)
HBM = pl.BlockSpec(memory_space=pltpu.HBM)
DENSE = jax.ShapeDtypeStruct((32, ZONES), F32)
X_FACES = [jax.ShapeDtypeStruct((72, 128), F32)] * 2
X_TWICE = [jax.ShapeDtypeStruct((144, 128), F32)] * 2
Y_FACES = [jax.ShapeDtypeStruct((36, 128), F32)] * 2
SLOT3 = jax.ShapeDtypeStruct((4, 32, SLOTS), F32)


def call(kernel, outs, args, scratch=(), flops=0, in_spec=VMEM, out_spec=VMEM):
    moved = 4 * sum(int(np.prod(a.shape)) for a in list(args) + list(outs))
    return pl.pallas_call(
        kernel,
        out_shape=outs,
        in_specs=[in_spec] * len(args),
        out_specs=[out_spec] * len(outs),
        scratch_shapes=list(scratch),
        compiler_params=pltpu.CompilerParams(vmem_limit_bytes=48 * 1024 * 1024),
        cost_estimate=pl.CostEstimate(flops=flops, bytes_accessed=moved, transcendentals=0),
    )(*args)


def exchange_x(low, high):
    n = lax.axis_size("gx")
    below = lax.ppermute(high, "gx", [(i, i + 1) for i in range(n - 1)])
    above = lax.ppermute(low, "gx", [(i + 1, i) for i in range(n - 1)])
    return below, above


def exchange_y(low, high):
    n = lax.axis_size("yz")
    below = lax.ppermute(high, "yz", [(i, (i + 1) % n) for i in range(n)])
    above = lax.ppermute(low, "yz", [(i, (i - 1) % n) for i in range(n)])
    return below, above


def on_device(
    state, mix_weights, mix_frac, mix_index, mix_count, vol_matrix, face_matrix, mat_matrix
):
    flat = state.reshape(27 * ROWS, CZ)
    small = [
        mix_weights.reshape(4, 27, SLOTS).transpose(1, 0, 2),
        mix_frac.reshape(4, SLOTS),
        mix_index.reshape(1, SLOTS),
        vol_matrix,
        face_matrix,
        mat_matrix.transpose(1, 0, 2),
        jnp.asarray(selections()),
    ]
    slot = lax.broadcasted_iota(jnp.int32, (1, SLOTS), 1)
    live = jnp.where(slot < mix_count.reshape(1, 1), 1.0, 0.0)
    g_space = pltpu.VMEM((224, ZONES), F32)
    pad = pltpu.VMEM((16, 3072), F32)
    bf = lambda rows, lanes: jax.ShapeDtypeStruct((rows, lanes), BF16)
    f32 = lambda rows, lanes: jax.ShapeDtypeStruct((rows, lanes), F32)

    v0, *out = call(
        first_kernel,
        [DENSE] + Y_FACES + [jax.ShapeDtypeStruct(a.shape, a.dtype) for a in small],
        [pltpu.with_memory_space_constraint(a, pltpu.HBM) for a in [flat] + small],
        [pltpu.VMEM((27 * ROWS, CZ), F32), pltpu.SemaphoreType.DMA((8,))],
        in_spec=HBM,
    )
    halo = exchange_y(*out[:2])
    weights, frac, idx, *_ = small = out[2:]
    inner, u, fm, wg, fh, fs, power = call(
        mixed_kernel,
        [DENSE, DENSE, f32(8, ZONES), bf(224, 128), bf(128, 64), bf(32, 256), f32(128, 128)],
        [live, v0] + small,
        [g_space, pltpu.VMEM((32, 128), F32), pltpu.VMEM((128, 128), F32),
         pltpu.VMEM((32, SLOTS), F32)],
        flops=3 * 10**9,
    )
    inner, *faces = call(
        y_first_kernel, [DENSE] + X_TWICE, [inner, u, v0, fh, *halo], [pad]
    )
    halo = exchange_x(*faces)
    c2, c3, pp, b3 = call(
        later_kernel, [DENSE, DENSE, bf(128, 256), SLOT3],
        [live, faces[0], power, weights, frac, idx], [pltpu.VMEM((32, SLOTS), F32)],
        flops=2 * 10**9,
    )
    v1, r0, beside, *faces = call(
        x_first_kernel, [DENSE, DENSE, f32(16, 2048)] + Y_FACES, [inner, u, v0, fh, *halo],
        [pad, pltpu.VMEM((16, 2048), F32)],
    )
    halo = exchange_y(*faces)
    inner, u = call(
        between_one, [DENSE, DENSE],
        [v0, v1, r0, beside, c2, fm, wg, fh, pp], [g_space], flops=2 * 10**9,
    )
    v2, r1, *faces = call(
        second_kernel, [DENSE, DENSE] + X_FACES + Y_FACES, [inner, u, fh, *halo], [pad]
    )
    x_halo = exchange_x(*faces[:2])
    y_halo = exchange_y(*faces[2:])
    u, slots = call(
        between_two, [DENSE, jax.ShapeDtypeStruct((27, 4, SLOTS), F32)],
        [v0, v2, r0, r1, c3, fm, live, idx, wg, pp, b3, weights], [g_space, pltpu.VMEM((32, ZONES), F32)],
        flops=2 * 10**9,
    )
    field, out = call(
        last_kernel,
        [jax.ShapeDtypeStruct((27 * ROWS, CZ), F32), jax.ShapeDtypeStruct((27, 4, SLOTS), F32)],
        [live, u, fh, fs, *y_halo, *x_halo, idx, slots],
        [pad, pltpu.VMEM((32, ZONES), F32), pltpu.VMEM((27 * ROWS, CZ), F32),
         pltpu.VMEM((27, 4, SLOTS), F32), pltpu.SemaphoreType.DMA((2,))],
        out_spec=ANY,
    )
    return field.reshape(state.shape), out.transpose(1, 0, 2).reshape(mix_weights.shape)


def solution(mesh):
    placed = (
        P(None, "gx", "yz", None),
        P("gx", "yz", None, None, None),
        P("gx", "yz", None, None),
        P("gx", "yz", None),
        P("gx", "yz"),
        P(),
        P(),
        P(),
    )
    return jax.shard_map(
        on_device,
        mesh=mesh,
        in_specs=placed,
        out_specs=(P(None, "gx", "yz", None), P("gx", "yz", None, None, None)),
        check_vma=False,
    )
```

```python
import numpy as np
import jax
import jax.numpy as jnp
from jax import lax
from jax.experimental import pallas as pl
from jax.experimental.pallas import tpu as pltpu
from jax.sharding import PartitionSpec as P

F32 = jnp.float32
BF16 = jnp.bfloat16
CX, CY, CZ = 4, 8, 128
ROWS = CX * CY
ZONES = ROWS * CZ
SLOTS = 1024
GROUP = 256
GROUPS = ZONES // GROUP


def face_dofs(face, own):
    axis, high = divmod(face, 2)
    at = (2 if high else 0) if own else (0 if high else 2)
    dofs = []
    for p in range(3):
        for q in range(3):
            abc = [p, q]
            abc.insert(axis, at)
            dofs.append(abc[0] * 9 + abc[1] * 3 + abc[2])
    return dofs


def selections():
    sel = np.zeros((64, 7 * 128 + 2 * 256), np.float32)
    for face in range(6):
        for q in range(9):
            row = 9 * face + q
            for copy in range(4):
                sel[row, copy * 32 + face_dofs(face, True)[q]] -= 1.0
                sel[row, (face + 1) * 128 + copy * 32 + face_dofs(face, False)[q]] += 1.0
                if face < 4:
                    sel[row, 7 * 128 + face * 64 + copy * 16 + q] += 1.0
                    sel[row, 9 * 128 + copy * 64 + face * 16 + q] += 1.0
    return sel


def halves(x):
    hi = x.astype(BF16)
    lo = (x - hi.astype(F32)).astype(BF16)
    return hi, lo


def stack_right(x):
    hi, lo = halves(x)
    return jnp.concatenate([hi, lo, hi, lo], axis=0)


def stack_left(x, half):
    hi = x.astype(BF16).astype(F32)
    lane = lax.broadcasted_iota(jnp.int32, x.shape, 1)
    return jnp.where(lane < half, hi, x - hi).astype(BF16)


def dot(a, b):
    return jnp.dot(a, b, preferred_element_type=F32)


def product(a, b):
    a_hi, a_lo = halves(a)
    b_hi, b_lo = halves(b)
    left = jnp.concatenate([a_hi, a_lo], axis=1)
    return dot(left, jnp.concatenate([b_hi, b_hi], axis=0)) + dot(a_hi, b_lo)


def block(r):
    return slice(r * CZ, (r + 1) * CZ)


def interior(v_ref, wg_ref, g_ref, out_ref, planes=tuple(range(CX)), shift=0):
    for x in range(CX):
        cols = slice(x * 1024, (x + 1) * 1024)
        right = stack_right(v_ref[:, cols])
        if x in planes:
            g_ref[:, cols] = dot(wg_ref[...], right)
        else:
            if x + 1 in planes:
                g_ref[32:64, cols] = dot(wg_ref[32:64, :], right)
            if x - 1 in planes:
                g_ref[64:96, cols] = dot(wg_ref[64:96, :], right)
    lane = lax.broadcasted_iota(jnp.int32, (32, CZ), 1)
    for x in planes:
        for y in range(CY):
            r = x * CY + y
            total = g_ref[0:32, block(r)]
            if x > 0:
                total += g_ref[32:64, block(r - CY)]
            if x < CX - 1:
                total += g_ref[64:96, block(r + CY)]
            if y > 0:
                total += g_ref[96:128, block(r - 1)]
            if y < CY - 1:
                total += g_ref[128:160, block(r + 1)]
            below = pltpu.roll(g_ref[160:192, block(r)], 1, 1)
            above = pltpu.roll(g_ref[192:224, block(r)], CZ - 1, 1)
            total += jnp.where(lane == 0, 0.0, below)
            total += jnp.where(lane == CZ - 1, 0.0, above)
            out_ref[:, block(r - shift)] = total


def lane_hot(idx):
    place = lax.broadcasted_iota(jnp.int32, (GROUP, SLOTS), 0)
    return jnp.where(place == (idx & (GROUP - 1)), 1.0, 0.0).astype(BF16)


def to_slots(r_ref, hot, idx):
    group = lax.shift_right_logical(idx, 8)
    parts = []
    for g in range(GROUPS):
        parts += halves(r_ref[:, g * GROUP:(g + 1) * GROUP])
    taken = dot(jnp.concatenate(parts, axis=0), hot)
    total = jnp.zeros((32, SLOTS), F32)
    for g in range(GROUPS):
        both = taken[64 * g:64 * g + 32] + taken[64 * g + 32:64 * g + 64]
        total = jnp.where(group == g, both, total)
    return total


def first_kernel(*refs):
    count = 8
    sources, (v_ref, ylo_ref, yhi_ref), rest = refs[:count], refs[count:count + 3], refs[count + 3:]
    targets, (state_ref, sems) = rest[:count - 1], rest[count - 1:]
    copies = [
        pltpu.make_async_copy(source, target, sems.at[k])
        for k, (source, target) in enumerate(zip(sources, (state_ref,) + targets))
    ]
    for copy in copies:
        copy.start()
    v_ref[24:32, :] = jnp.zeros((8, ZONES), F32)
    copies[0].wait()
    for q in range(9):
        low, high = face_dofs(2, True)[q], face_dofs(3, True)[q]
        ylo_ref[q * 4:q * 4 + 4, :] = state_ref[pl.ds(low * 32, 4, stride=8), :]
        yhi_ref[q * 4:q * 4 + 4, :] = state_ref[pl.ds(high * 32 + 7, 4, stride=8), :]
    for r in range(ROWS):
        v_ref[0:27, block(r)] = state_ref[pl.ds(r, 27, stride=32), :]
    for copy in copies[1:]:
        copy.wait()


def mixed_kernel(
    live_ref, v_ref, w_ref, frac_ref, idx_ref, vol_ref, face_ref, mat_ref, sel_ref,
    int_ref, u_ref, fm_ref, wg_ref, fh_ref, fs_ref, power_ref, first_ref,
    g_ref, small_ref, diag_ref, wpad_ref,
):
    small_ref[...] = jnp.zeros((32, 128), F32)
    small_ref[0:27, 0:54] = face_ref[...]
    f_hi, f_lo = halves(small_ref[:, 0:64])
    sel = sel_ref[...].astype(BF16)
    laid = dot(f_hi, sel) + dot(f_lo, sel)
    small_ref[...] = jnp.zeros((32, 128), F32)
    small_ref[0:27, 0:27] = vol_ref[...]
    vol = small_ref[...]
    vol4 = vol + pltpu.roll(vol, 32, 1)
    vol4 = vol4 + pltpu.roll(vol4, 64, 1)
    wg_ref[0:32, :] = stack_left(laid[:, 0:128] + vol4, 64)
    for k in range(1, 7):
        wg_ref[32 * k:32 * k + 32, :] = stack_left(laid[:, 128 * k:128 * k + 128], 64)
    for k in range(4):
        first = 7 * 128 + 64 * k
        fh_ref[32 * k:32 * k + 32, :] = stack_left(laid[:, first:first + 64], 32)
    fs_ref[...] = stack_left(laid[:, 9 * 128:11 * 128], 128)
    int_ref[:, 1024:3072] = jnp.zeros((32, 2048), F32)
    interior(v_ref, wg_ref, g_ref, int_ref, (0, 3))

    for m in range(4):
        small_ref[0:27, 0:27] = mat_ref[:, m, :]
        small = small_ref[...]
        diag_ref[32 * m:32 * m + 32, :] = pltpu.roll(small, 32 * m, 1) if m else small
    m1 = diag_ref[...]
    m2 = product(m1, m1)
    p1 = identity() + m1 + m2 + product(m1 + m2, m2)
    power_ref[...] = p1

    idx = idx_ref[...]
    frac = frac_ref[...]
    wpad_ref[...] = jnp.zeros((32, SLOTS), F32)
    first = 0.0
    for m in range(4):
        wpad_ref[0:27, :] = w_ref[:, m, :]
        values = dot(stacked(p1, m), stack_right(wpad_ref[...]))
        first = first + frac[m:m + 1, :] * values
    live = live_ref[...] > 0.0
    first = jnp.where(live, first, 0.0)
    first = jnp.concatenate([first[0:27], jnp.where(live, frac, 0.0), first[31:32]], axis=0)

    first_ref[...] = first
    groups = (0, 1, 2, 3, 12, 13, 14, 15)
    for g, here in zip(groups, to_zones(first, lane_hot(idx), idx, groups)):
        cols = slice(g * GROUP, (g + 1) * GROUP)
        u_ref[:, cols] = jnp.where(here[27:28] > 0.0, here, v_ref[:, cols])
        fm_ref[:, cols] = here[24:32]


def identity():
    row = lax.broadcasted_iota(jnp.int32, (128, 128), 0)
    column = lax.broadcasted_iota(jnp.int32, (128, 128), 1)
    return jnp.where(row == column, 1.0, 0.0)


def stacked(matrix, m):
    rows = matrix[32 * m:32 * m + 32, :]
    for shift in (32, 64):
        rows = rows + pltpu.roll(rows, shift, 1)
    return stack_left(rows, 64)


def to_zones(values, hot, idx, groups=tuple(range(GROUPS))):
    both = jnp.concatenate(halves(values), axis=0)
    group = lax.shift_right_logical(idx, 8)
    parts = [both * jnp.where(group == g, 1.0, 0.0).astype(BF16) for g in groups]
    dense = lax.dot_general(
        jnp.concatenate(parts, axis=0), hot, (((1,), (1,)), ((), ())), preferred_element_type=F32
    )
    rows = values.shape[0]
    return [
        dense[2 * rows * g:2 * rows * g + rows] + dense[2 * rows * g + rows:2 * rows * (g + 1)]
        for g in range(len(groups))
    ]


def later_kernel(
    live_ref, after_ref, power_ref, w_ref, frac_ref, idx_ref, v_ref, wg_ref, first_ref,
    c2_ref, c3_ref, pp_ref, b3_ref, mid_ref, u_mid_ref, fm_mid_ref, wpad_ref, g_ref,
):
    interior(v_ref, wg_ref, g_ref, mid_ref, (1, 2), CY)
    eye = identity()
    p1 = power_ref[...]
    p2 = product(p1, p1)
    q2 = 0.75 * eye + 0.25 * p2
    q3 = (1.0 / 3.0) * eye + 0.5 * p1 + (1.0 / 6.0) * product(p2, p1)
    frac = frac_ref[...]
    wpad_ref[...] = jnp.zeros((32, SLOTS), F32)
    total = 0.0
    for m in range(4):
        pp_ref[32 * m:32 * m + 32, 0:128] = stacked(p1, m)
        pp_ref[32 * m:32 * m + 32, 128:256] = stacked(p2, m)
        wpad_ref[0:27, :] = w_ref[:, m, :]
        left = jnp.concatenate([stacked(q2, m), stacked(q3, m)], axis=0)
        values = dot(left, stack_right(wpad_ref[...]))
        b3_ref[m] = values[32:64]
        total = total + frac[m:m + 1, :] * values
    idx = idx_ref[...]
    hot = lane_hot(idx)
    groups = tuple(range(4, 12))
    for g, here in zip(groups, to_zones(first_ref[...], hot, idx, groups)):
        cols = slice((g - 4) * GROUP, (g - 3) * GROUP)
        old = v_ref[:, g * GROUP:(g + 1) * GROUP]
        u_mid_ref[:, cols] = jnp.where(here[27:28] > 0.0, here, old)
        fm_mid_ref[:, cols] = here[24:32]
    dense = to_zones(jnp.where(live_ref[...] > 0.0, total, 0.0), hot, idx)
    for g in range(GROUPS):
        cols = slice(g * GROUP, (g + 1) * GROUP)
        c2_ref[:, cols] = dense[g][0:32]
        c3_ref[:, cols] = dense[g][32:64]


def inside(axis):
    at = lax.axis_index(axis)
    return at > 0, at < lax.axis_size(axis) - 1


def halo_x(xlo_ref, xhi_ref, pad_ref, first=0):
    for y in range(CY):
        pad_ref[0:9, block(y)] = xlo_ref[pl.ds(first + y, 9, stride=8), :]
        pad_ref[0:9, block(CY + y)] = xhi_ref[pl.ds(first + y, 9, stride=8), :]


def halo_y(ylo_ref, yhi_ref, pad_ref):
    low, high = inside("yz")
    for x in range(CX):
        pad_ref[0:9, block(16 + x)] = jnp.where(low, ylo_ref[pl.ds(x, 9, stride=4), :], 0.0)
        pad_ref[0:9, block(20 + x)] = jnp.where(high, yhi_ref[pl.ds(x, 9, stride=4), :], 0.0)


def terms(fh_ref, pad_ref, face):
    first, last = ((0, 1024), (1024, 2048), (2048, 2560), (2560, 3072))[face]
    return dot(fh_ref[32 * face:32 * face + 32, :], stack_right(pad_ref[:, first:last]))


def halo_add(int_ref, fh_ref, pad_ref, rate_ref, along_x, along_y):
    x_low, x_high = [terms(fh_ref, pad_ref, face) for face in (0, 1)] if along_x else (None, None)
    y_low, y_high = [terms(fh_ref, pad_ref, face) for face in (2, 3)] if along_y else (None, None)
    for x in range(CX):
        for y in range(CY):
            r = x * CY + y
            total = int_ref[:, block(r)]
            if along_x and x == 0:
                total += x_low[:, block(y)]
            if along_x and x == CX - 1:
                total += x_high[:, block(y)]
            if along_y and y == 0:
                total += y_low[:, block(x)]
            if along_y and y == CY - 1:
                total += y_high[:, block(x)]
            rate_ref[:, block(r)] = total


def x_faces(v_ref, xlo_ref, xhi_ref, first=0):
    for y in range(CY):
        xlo_ref[pl.ds(first + y, 9, stride=8), :] = v_ref[0:9, block(y)]
        xhi_ref[pl.ds(first + y, 9, stride=8), :] = v_ref[18:27, block(24 + y)]


def y_faces(v_ref, ylo_ref, yhi_ref):
    for x in range(CX):
        for a in range(3):
            ylo_ref[pl.ds(12 * a + x, 3, stride=4), :] = v_ref[9 * a:9 * a + 3, block(8 * x)]
            yhi_ref[pl.ds(12 * a + x, 3, stride=4), :] = v_ref[9 * a + 6:9 * a + 9, block(8 * x + 7)]


def y_first_kernel(
    int_ref, u_ref, v_ref, fh_ref, yl_ref, yh_ref, rate_ref, xlo_ref, xhi_ref, pad_ref,
):
    pad_ref[...] = jnp.zeros((16, 3072), F32)
    halo_y(yl_ref, yh_ref, pad_ref)
    halo_add(int_ref, fh_ref, pad_ref, rate_ref, False, True)
    x_faces(v_ref, xlo_ref, xhi_ref)
    for y in range(CY):
        xlo_ref[pl.ds(72 + y, 9, stride=8), :] = u_ref[0:9, block(y)] + rate_ref[0:9, block(y)]
        xhi_ref[pl.ds(72 + y, 9, stride=8), :] = (
            u_ref[18:27, block(24 + y)] + rate_ref[18:27, block(24 + y)]
        )


def x_first_kernel(
    int_ref, mid_ref, u_ref, u_mid_ref, fm_ref, fm_mid_ref, v_ref, fh_ref, xl_ref, xh_ref,
    next_ref, rate_ref, beside_ref, f_ref, ylo_ref, yhi_ref, pad_ref, own_ref,
):
    pad_ref[...] = jnp.zeros((16, 3072), F32)
    halo_x(xl_ref, xh_ref, pad_ref)
    halo_add(int_ref, fh_ref, pad_ref, rate_ref, True, False)
    rate_ref[:, 1024:3072] += mid_ref[...]
    for x in range(CX):
        cols = slice(x * 1024, (x + 1) * 1024)
        inner = slice((x - 1) * 1024, x * 1024)
        u = u_mid_ref[:, inner] if x in (1, 2) else u_ref[:, cols]
        next_ref[:, cols] = u + rate_ref[:, cols]
        f_ref[:, cols] = fm_mid_ref[:, inner] if x in (1, 2) else fm_ref[:, cols]
    y_faces(next_ref, ylo_ref, yhi_ref)
    own_ref[...] = jnp.zeros((16, 2048), F32)
    own_ref[0:9, 0:1024] = v_ref[0:9, 0:1024]
    own_ref[0:9, 1024:2048] = v_ref[18:27, 3072:4096]
    to_low = dot(fh_ref[32:64, :], stack_right(own_ref[:, 0:1024]))
    to_high = dot(fh_ref[0:32, :], stack_right(own_ref[:, 1024:2048]))
    low, high = inside("gx")
    halo_x(xl_ref, xh_ref, pad_ref, 72)
    beside_ref[...] = jnp.zeros((16, 2048), F32)
    beside_ref[0:9, 0:1024] = pad_ref[0:9, 0:1024] + jnp.where(low, to_low[18:27], 0.0)
    beside_ref[0:9, 1024:2048] = pad_ref[0:9, 1024:2048] + jnp.where(high, to_high[0:9], 0.0)


def second_kernel(
    int_ref, u_ref, fh_ref, yl_ref, yh_ref,
    v_ref, rate_ref, xlo_ref, xhi_ref, ylo_ref, yhi_ref, pad_ref,
):
    pad_ref[...] = jnp.zeros((16, 3072), F32)
    halo_y(yl_ref, yh_ref, pad_ref)
    halo_add(int_ref, fh_ref, pad_ref, rate_ref, False, True)
    v_ref[...] = u_ref[...] + 0.25 * rate_ref[...]
    x_faces(v_ref, xlo_ref, xhi_ref)
    y_faces(v_ref, ylo_ref, yhi_ref)


def weighted(f, q):
    return sum(f[m + 3:m + 4] * q[32 * m:32 * m + 32] for m in range(4))


def between_one(
    v0_ref, v1_ref, r_ref, beside_ref, c2_ref, fm_ref, wg_ref, fh_ref, pp_ref,
    int_ref, u_ref, g_ref,
):
    interior(v1_ref, wg_ref, g_ref, int_ref)
    int_ref[:, 0:1024] += terms(fh_ref, beside_ref, 0)
    int_ref[:, 3072:4096] += terms(fh_ref, beside_ref, 1)
    for x in range(CX):
        cols = slice(x * 1024, (x + 1) * 1024)
        f = fm_ref[:, cols]
        s1 = weighted(f, dot(pp_ref[:, 0:128], stack_right(r_ref[:, cols])))
        bulk = 0.75 * v0_ref[:, cols] + 0.25 * v1_ref[:, cols]
        u_ref[:, cols] = jnp.where(f[3:4] > 0.0, c2_ref[:, cols] + 0.25 * s1, bulk)


def between_two(
    v0_ref, v2_ref, r0_ref, r1_ref, c3_ref, fm_ref, live_ref, idx_ref, wg_ref, pp_ref, b3_ref, w_ref,
    u_ref, slots_ref, g_ref, int_ref,
):
    interior(v2_ref, wg_ref, g_ref, int_ref)
    for x in range(CX):
        cols = slice(x * 1024, (x + 1) * 1024)
        both = jnp.concatenate([stack_right(r1_ref[:, cols]), stack_right(r0_ref[:, cols])], axis=0)
        f = fm_ref[:, cols]
        s1 = weighted(f, dot(pp_ref[...], both))
        bulk = (1.0 / 3.0) * v0_ref[:, cols] + (2.0 / 3.0) * v2_ref[:, cols]
        old = jnp.where(f[3:4] > 0.0, c3_ref[:, cols] + (1.0 / 6.0) * s1, bulk)
        u_ref[:, cols] = old + (2.0 / 3.0) * int_ref[:, cols]
    idx = idx_ref[...]
    hot = lane_hot(idx)
    both = jnp.concatenate(
        [stack_right(to_slots(r1_ref, hot, idx)), stack_right(to_slots(r0_ref, hot, idx))], axis=0
    )
    inner = (2.0 / 3.0) * to_slots(int_ref, hot, idx)
    live = live_ref[...] > 0.0
    for m in range(4):
        value = b3_ref[m] + inner + (1.0 / 6.0) * dot(pp_ref[32 * m:32 * m + 32, :], both)
        slots_ref[:, m, :] = jnp.where(live, value[0:27], w_ref[:, m, :])


def faces_to_slots(pad_ref, idx):
    parts = []
    for g in range(8):
        parts += halves(pad_ref[:, g * GROUP:(g + 1) * GROUP])
    for x in range(CX):
        low, high = pad_ref[:, block(16 + x)], pad_ref[:, block(20 + x)]
        parts += halves(jnp.concatenate([low, high], axis=1))
    taken = dot(jnp.concatenate(parts, axis=0), lane_hot(idx))
    taken = [taken[32 * k:32 * k + 16] + taken[32 * k + 16:32 * k + 32] for k in range(12)]
    group = lax.shift_right_logical(idx, 8)
    x, y = lax.shift_right_logical(idx, 10), lax.shift_right_logical(idx, 7) & 7
    x_low = x_high = beside = jnp.zeros((16, SLOTS), F32)
    for k in range(4):
        x_low = jnp.where(group == k, taken[k], x_low)
        x_high = jnp.where(group == 12 + k, taken[4 + k], x_high)
        beside = jnp.where(x == k, taken[8 + k], beside)
    y_low, y_high = jnp.where(y == 0, beside, 0.0), jnp.where(y == CY - 1, beside, 0.0)
    return jnp.concatenate([x_low, x_high, y_low, y_high], axis=0)


def last_kernel(
    live_ref, u_ref, fh_ref, fs_ref, yl_ref, yh_ref, xl_ref, xh_ref, idx_ref, slots_ref,
    field_hbm, out_hbm, pad_ref, whole_ref, field_ref, out_ref, sems,
):
    pad_ref[...] = jnp.zeros((16, 3072), F32)
    halo_x(xl_ref, xh_ref, pad_ref)
    halo_y(yl_ref, yh_ref, pad_ref)
    pad_ref[...] = (2.0 / 3.0) * pad_ref[...]
    halo_add(u_ref, fh_ref, pad_ref, whole_ref, True, True)
    for r in range(ROWS):
        field_ref[pl.ds(r, 27, stride=32), :] = whole_ref[0:27, block(r)]
    field_copy = pltpu.make_async_copy(field_ref, field_hbm, sems.at[0])
    field_copy.start()
    added = dot(fs_ref[...], stack_right(faces_to_slots(pad_ref, idx_ref[...])))
    added = jnp.where(live_ref[...] > 0.0, added, 0.0)
    for d in range(27):
        out_ref[d] = slots_ref[d] + added[d:d + 1]
    out_copy = pltpu.make_async_copy(out_ref, out_hbm, sems.at[1])
    out_copy.start()
    field_copy.wait()
    out_copy.wait()


VMEM = pl.BlockSpec(memory_space=pltpu.VMEM)
ANY = pl.BlockSpec(memory_space=pl.ANY)
HBM = pl.BlockSpec(memory_space=pltpu.HBM)
DENSE = jax.ShapeDtypeStruct((32, ZONES), F32)
X_FACES = [jax.ShapeDtypeStruct((72, 128), F32)] * 2
X_TWICE = [jax.ShapeDtypeStruct((144, 128), F32)] * 2
Y_FACES = [jax.ShapeDtypeStruct((36, 128), F32)] * 2
SLOT3 = jax.ShapeDtypeStruct((4, 32, SLOTS), F32)


def call(kernel, outs, args, scratch=(), flops=0, in_spec=VMEM, out_spec=VMEM):
    moved = 4 * sum(int(np.prod(a.shape)) for a in list(args) + list(outs))
    return pl.pallas_call(
        kernel,
        out_shape=outs,
        in_specs=[in_spec] * len(args),
        out_specs=[out_spec] * len(outs),
        scratch_shapes=list(scratch),
        compiler_params=pltpu.CompilerParams(vmem_limit_bytes=48 * 1024 * 1024),
        cost_estimate=pl.CostEstimate(flops=flops, bytes_accessed=moved, transcendentals=0),
    )(*args)


def exchange_x(low, high):
    n = lax.axis_size("gx")
    below = lax.ppermute(high, "gx", [(i, i + 1) for i in range(n - 1)])
    above = lax.ppermute(low, "gx", [(i + 1, i) for i in range(n - 1)])
    return below, above


def exchange_y(low, high):
    n = lax.axis_size("yz")
    below = lax.ppermute(high, "yz", [(i, (i + 1) % n) for i in range(n)])
    above = lax.ppermute(low, "yz", [(i, (i - 1) % n) for i in range(n)])
    return below, above


def on_device(
    state, mix_weights, mix_frac, mix_index, mix_count, vol_matrix, face_matrix, mat_matrix
):
    flat = state.reshape(27 * ROWS, CZ)
    small = [
        mix_weights.reshape(4, 27, SLOTS).transpose(1, 0, 2),
        mix_frac.reshape(4, SLOTS),
        mix_index.reshape(1, SLOTS),
        vol_matrix,
        face_matrix,
        mat_matrix.transpose(1, 0, 2),
        jnp.asarray(selections()),
    ]
    slot = lax.broadcasted_iota(jnp.int32, (1, SLOTS), 1)
    live = jnp.where(slot < mix_count.reshape(1, 1), 1.0, 0.0)
    g_space = pltpu.VMEM((224, ZONES), F32)
    pad = pltpu.VMEM((16, 3072), F32)
    bf = lambda rows, lanes: jax.ShapeDtypeStruct((rows, lanes), BF16)
    f32 = lambda rows, lanes: jax.ShapeDtypeStruct((rows, lanes), F32)

    v0, *out = call(
        first_kernel,
        [DENSE] + Y_FACES + [jax.ShapeDtypeStruct(a.shape, a.dtype) for a in small],
        [pltpu.with_memory_space_constraint(a, pltpu.HBM) for a in [flat] + small],
        [pltpu.VMEM((27 * ROWS, CZ), F32), pltpu.SemaphoreType.DMA((8,))],
        in_spec=HBM,
    )
    halo = exchange_y(*out[:2])
    weights, frac, idx, *_ = small = out[2:]
    inner, u, fm, wg, fh, fs, power, first = call(
        mixed_kernel,
        [DENSE, DENSE, f32(8, ZONES), bf(224, 128), bf(128, 64), bf(32, 256), f32(128, 128),
         f32(32, SLOTS)],
        [live, v0] + small,
        [g_space, pltpu.VMEM((32, 128), F32), pltpu.VMEM((128, 128), F32),
         pltpu.VMEM((32, SLOTS), F32)],
        flops=3 * 10**9,
    )
    inner, *faces = call(
        y_first_kernel, [DENSE] + X_TWICE, [inner, u, v0, fh, *halo], [pad]
    )
    halo = exchange_x(*faces)
    c2, c3, pp, b3, mid, u_mid, fm_mid = call(
        later_kernel,
        [DENSE, DENSE, bf(128, 256), SLOT3, f32(32, 2048), f32(32, 2048), f32(8, 2048)],
        [live, faces[0], power, weights, frac, idx, v0, wg, first],
        [pltpu.VMEM((32, SLOTS), F32), g_space],
        flops=2 * 10**9,
    )
    v1, r0, beside, fm, *faces = call(
        x_first_kernel, [DENSE, DENSE, f32(16, 2048), f32(8, ZONES)] + Y_FACES,
        [inner, mid, u, u_mid, fm, fm_mid, v0, fh, *halo],
        [pad, pltpu.VMEM((16, 2048), F32)],
    )
    halo = exchange_y(*faces)
    inner, u = call(
        between_one, [DENSE, DENSE],
        [v0, v1, r0, beside, c2, fm, wg, fh, pp], [g_space], flops=2 * 10**9,
    )
    v2, r1, *faces = call(
        second_kernel, [DENSE, DENSE] + X_FACES + Y_FACES, [inner, u, fh, *halo], [pad]
    )
    x_halo = exchange_x(*faces[:2])
    y_halo = exchange_y(*faces[2:])
    u, slots = call(
        between_two, [DENSE, jax.ShapeDtypeStruct((27, 4, SLOTS), F32)],
        [v0, v2, r0, r1, c3, fm, live, idx, wg, pp, b3, weights], [g_space, pltpu.VMEM((32, ZONES), F32)],
        flops=2 * 10**9,
    )
    field, out = call(
        last_kernel,
        [jax.ShapeDtypeStruct((27 * ROWS, CZ), F32), jax.ShapeDtypeStruct((27, 4, SLOTS), F32)],
        [live, u, fh, fs, *y_halo, *x_halo, idx, slots],
        [pad, pltpu.VMEM((32, ZONES), F32), pltpu.VMEM((27 * ROWS, CZ), F32),
         pltpu.VMEM((27, 4, SLOTS), F32), pltpu.SemaphoreType.DMA((2,))],
        out_spec=ANY,
    )
    return field.reshape(state.shape), out.transpose(1, 0, 2).reshape(mix_weights.shape)


def solution(mesh):
    placed = (
        P(None, "gx", "yz", None),
        P("gx", "yz", None, None, None),
        P("gx", "yz", None, None),
        P("gx", "yz", None),
        P("gx", "yz"),
        P(),
        P(),
        P(),
    )
    return jax.shard_map(
        on_device,
        mesh=mesh,
        in_specs=placed,
        out_specs=(P(None, "gx", "yz", None), P("gx", "yz", None, None, None)),
        check_vma=False,
    )
```

```python
import numpy as np
import jax
import jax.numpy as jnp
from jax import lax
from jax.experimental import pallas as pl
from jax.experimental.pallas import tpu as pltpu
from jax.sharding import PartitionSpec as P

F32 = jnp.float32
BF16 = jnp.bfloat16
CX, CY, CZ = 4, 8, 128
ROWS = CX * CY
ZONES = ROWS * CZ
SLOTS = 1024
GROUP = 256
GROUPS = ZONES // GROUP


def face_dofs(face, own):
    axis, high = divmod(face, 2)
    at = (2 if high else 0) if own else (0 if high else 2)
    dofs = []
    for p in range(3):
        for q in range(3):
            abc = [p, q]
            abc.insert(axis, at)
            dofs.append(abc[0] * 9 + abc[1] * 3 + abc[2])
    return dofs


def selections():
    sel = np.zeros((64, 7 * 128 + 2 * 256), np.float32)
    for face in range(6):
        for q in range(9):
            row = 9 * face + q
            for copy in range(4):
                sel[row, copy * 32 + face_dofs(face, True)[q]] -= 1.0
                sel[row, (face + 1) * 128 + copy * 32 + face_dofs(face, False)[q]] += 1.0
                if face < 4:
                    sel[row, 7 * 128 + face * 64 + copy * 16 + q] += 1.0
                    sel[row, 9 * 128 + copy * 64 + face * 16 + q] += 1.0
    return sel


def halves(x):
    hi = x.astype(BF16)
    lo = (x - hi.astype(F32)).astype(BF16)
    return hi, lo


def stack_right(x):
    hi, lo = halves(x)
    return jnp.concatenate([hi, lo, hi, lo], axis=0)


def stack_left(x, half):
    hi = x.astype(BF16).astype(F32)
    lane = lax.broadcasted_iota(jnp.int32, x.shape, 1)
    return jnp.where(lane < half, hi, x - hi).astype(BF16)


def dot(a, b):
    return jnp.dot(a, b, preferred_element_type=F32)


def product(a, b):
    a_hi, a_lo = halves(a)
    b_hi, b_lo = halves(b)
    left = jnp.concatenate([a_hi, a_lo], axis=1)
    return dot(left, jnp.concatenate([b_hi, b_hi], axis=0)) + dot(a_hi, b_lo)


def block(r):
    return slice(r * CZ, (r + 1) * CZ)


def interior(v_ref, wg_ref, g_ref, out_ref, planes=tuple(range(CX)), shift=0):
    for x in range(CX):
        cols = slice(x * 1024, (x + 1) * 1024)
        right = stack_right(v_ref[:, cols])
        if x in planes:
            g_ref[:, cols] = dot(wg_ref[...], right)
        else:
            if x + 1 in planes:
                g_ref[32:64, cols] = dot(wg_ref[32:64, :], right)
            if x - 1 in planes:
                g_ref[64:96, cols] = dot(wg_ref[64:96, :], right)
    lane = lax.broadcasted_iota(jnp.int32, (32, CZ), 1)
    for x in planes:
        for y in range(CY):
            r = x * CY + y
            total = g_ref[0:32, block(r)]
            if x > 0:
                total += g_ref[32:64, block(r - CY)]
            if x < CX - 1:
                total += g_ref[64:96, block(r + CY)]
            if y > 0:
                total += g_ref[96:128, block(r - 1)]
            if y < CY - 1:
                total += g_ref[128:160, block(r + 1)]
            below = pltpu.roll(g_ref[160:192, block(r)], 1, 1)
            above = pltpu.roll(g_ref[192:224, block(r)], CZ - 1, 1)
            total += jnp.where(lane == 0, 0.0, below)
            total += jnp.where(lane == CZ - 1, 0.0, above)
            out_ref[:, block(r - shift)] = total


def lane_hot(idx):
    place = lax.broadcasted_iota(jnp.int32, (GROUP, SLOTS), 0)
    return jnp.where(place == (idx & (GROUP - 1)), 1.0, 0.0).astype(BF16)


def to_slots(r_ref, hot, idx):
    group = lax.shift_right_logical(idx, 8)
    parts = []
    for g in range(GROUPS):
        parts += halves(r_ref[:, g * GROUP:(g + 1) * GROUP])
    taken = dot(jnp.concatenate(parts, axis=0), hot)
    total = jnp.zeros((32, SLOTS), F32)
    for g in range(GROUPS):
        both = taken[64 * g:64 * g + 32] + taken[64 * g + 32:64 * g + 64]
        total = jnp.where(group == g, both, total)
    return total


def first_kernel(*refs):
    count = 8
    sources, (v_ref, ylo_ref, yhi_ref), rest = refs[:count], refs[count:count + 3], refs[count + 3:]
    targets, (state_ref, sems) = rest[:count - 1], rest[count - 1:]
    copies = [
        pltpu.make_async_copy(source, target, sems.at[k])
        for k, (source, target) in enumerate(zip(sources, (state_ref,) + targets))
    ]
    for copy in copies:
        copy.start()
    v_ref[24:32, :] = jnp.zeros((8, ZONES), F32)
    copies[0].wait()
    for q in range(9):
        low, high = face_dofs(2, True)[q], face_dofs(3, True)[q]
        ylo_ref[q * 4:q * 4 + 4, :] = state_ref[pl.ds(low * 32, 4, stride=8), :]
        yhi_ref[q * 4:q * 4 + 4, :] = state_ref[pl.ds(high * 32 + 7, 4, stride=8), :]
    for r in range(ROWS):
        v_ref[0:27, block(r)] = state_ref[pl.ds(r, 27, stride=32), :]
    for copy in copies[1:]:
        copy.wait()


def mixed_kernel(
    live_ref, v_ref, w_ref, frac_ref, idx_ref, vol_ref, face_ref, mat_ref, sel_ref,
    int_ref, u_ref, fm_ref, wg_ref, fh_ref, fs_ref, power_ref, first_ref,
    g_ref, small_ref, diag_ref, wpad_ref,
):
    small_ref[...] = jnp.zeros((32, 128), F32)
    small_ref[0:27, 0:54] = face_ref[...]
    f_hi, f_lo = halves(small_ref[:, 0:64])
    sel = sel_ref[...].astype(BF16)
    laid = dot(f_hi, sel) + dot(f_lo, sel)
    small_ref[...] = jnp.zeros((32, 128), F32)
    small_ref[0:27, 0:27] = vol_ref[...]
    vol = small_ref[...]
    vol4 = vol + pltpu.roll(vol, 32, 1)
    vol4 = vol4 + pltpu.roll(vol4, 64, 1)
    wg_ref[0:32, :] = stack_left(laid[:, 0:128] + vol4, 64)
    for k in range(1, 7):
        wg_ref[32 * k:32 * k + 32, :] = stack_left(laid[:, 128 * k:128 * k + 128], 64)
    for k in range(4):
        first = 7 * 128 + 64 * k
        fh_ref[32 * k:32 * k + 32, :] = stack_left(laid[:, first:first + 64], 32)
    fs_ref[...] = stack_left(laid[:, 9 * 128:11 * 128], 128)
    int_ref[:, 1024:3072] = jnp.zeros((32, 2048), F32)
    interior(v_ref, wg_ref, g_ref, int_ref, (0, 3))

    for m in range(4):
        small_ref[0:27, 0:27] = mat_ref[:, m, :]
        small = small_ref[...]
        diag_ref[32 * m:32 * m + 32, :] = pltpu.roll(small, 32 * m, 1) if m else small
    m1 = diag_ref[...]
    m2 = product(m1, m1)
    p1 = identity() + m1 + m2 + product(m1 + m2, m2)
    power_ref[...] = p1

    idx = idx_ref[...]
    frac = frac_ref[...]
    wpad_ref[...] = jnp.zeros((32, SLOTS), F32)
    first = 0.0
    for m in range(4):
        wpad_ref[0:27, :] = w_ref[:, m, :]
        values = dot(stacked(p1, m), stack_right(wpad_ref[...]))
        first = first + frac[m:m + 1, :] * values
    live = live_ref[...] > 0.0
    first = jnp.where(live, first, 0.0)
    first = jnp.concatenate([first[0:27], jnp.where(live, frac, 0.0), first[31:32]], axis=0)

    first_ref[...] = first
    groups = (0, 1, 2, 3, 12, 13, 14, 15)
    for g, here in zip(groups, to_zones(first, lane_hot(idx), idx, groups)):
        cols = slice(g * GROUP, (g + 1) * GROUP)
        u_ref[:, cols] = jnp.where(here[27:28] > 0.0, here, v_ref[:, cols])
        fm_ref[:, cols] = here[24:32]


def identity():
    row = lax.broadcasted_iota(jnp.int32, (128, 128), 0)
    column = lax.broadcasted_iota(jnp.int32, (128, 128), 1)
    return jnp.where(row == column, 1.0, 0.0)


def stacked(matrix, m):
    rows = matrix[32 * m:32 * m + 32, :]
    for shift in (32, 64):
        rows = rows + pltpu.roll(rows, shift, 1)
    return stack_left(rows, 64)


def to_zones(values, hot, idx, groups=tuple(range(GROUPS))):
    both = jnp.concatenate(halves(values), axis=0)
    group = lax.shift_right_logical(idx, 8)
    parts = [both * jnp.where(group == g, 1.0, 0.0).astype(BF16) for g in groups]
    dense = lax.dot_general(
        jnp.concatenate(parts, axis=0), hot, (((1,), (1,)), ((), ())), preferred_element_type=F32
    )
    rows = values.shape[0]
    return [
        dense[2 * rows * g:2 * rows * g + rows] + dense[2 * rows * g + rows:2 * rows * (g + 1)]
        for g in range(len(groups))
    ]


def later_kernel(
    live_ref, after_ref, power_ref, w_ref, frac_ref, idx_ref, v_ref, wg_ref, first_ref,
    c2_ref, c3_ref, pp_ref, b3_ref, mid_ref, u_mid_ref, fm_mid_ref, wpad_ref, g_ref,
):
    interior(v_ref, wg_ref, g_ref, mid_ref, (1, 2), CY)
    eye = identity()
    p1 = power_ref[...]
    p2 = product(p1, p1)
    q2 = 0.75 * eye + 0.25 * p2
    q3 = (1.0 / 3.0) * eye + 0.5 * p1 + (1.0 / 6.0) * product(p2, p1)
    frac = frac_ref[...]
    wpad_ref[...] = jnp.zeros((32, SLOTS), F32)
    total = 0.0
    for m in range(4):
        pp_ref[32 * m:32 * m + 32, 0:128] = stacked(p1, m)
        pp_ref[32 * m:32 * m + 32, 128:256] = stacked(p2, m)
        wpad_ref[0:27, :] = w_ref[:, m, :]
        left = jnp.concatenate([stacked(q2, m), stacked(q3, m)], axis=0)
        values = dot(left, stack_right(wpad_ref[...]))
        b3_ref[m] = values[32:64]
        total = total + frac[m:m + 1, :] * values
    idx = idx_ref[...]
    hot = lane_hot(idx)
    groups = tuple(range(4, 12))
    for g, here in zip(groups, to_zones(first_ref[...], hot, idx, groups)):
        cols = slice((g - 4) * GROUP, (g - 3) * GROUP)
        old = v_ref[:, g * GROUP:(g + 1) * GROUP]
        u_mid_ref[:, cols] = jnp.where(here[27:28] > 0.0, here, old)
        fm_mid_ref[:, cols] = here[24:32]
    dense = to_zones(jnp.where(live_ref[...] > 0.0, total, 0.0), hot, idx)
    for g in range(GROUPS):
        cols = slice(g * GROUP, (g + 1) * GROUP)
        c2_ref[:, cols] = dense[g][0:32]
        c3_ref[:, cols] = dense[g][32:64]


def inside(axis):
    at = lax.axis_index(axis)
    return at > 0, at < lax.axis_size(axis) - 1


def halo_x(xlo_ref, xhi_ref, pad_ref, first=0):
    for y in range(CY):
        pad_ref[0:9, block(y)] = xlo_ref[pl.ds(first + y, 9, stride=8), :]
        pad_ref[0:9, block(CY + y)] = xhi_ref[pl.ds(first + y, 9, stride=8), :]


def halo_y(ylo_ref, yhi_ref, pad_ref):
    low, high = inside("yz")
    for x in range(CX):
        pad_ref[0:9, block(16 + x)] = jnp.where(low, ylo_ref[pl.ds(x, 9, stride=4), :], 0.0)
        pad_ref[0:9, block(20 + x)] = jnp.where(high, yhi_ref[pl.ds(x, 9, stride=4), :], 0.0)


def terms(fh_ref, pad_ref, face):
    first, last = ((0, 1024), (1024, 2048), (2048, 2560), (2560, 3072))[face]
    return dot(fh_ref[32 * face:32 * face + 32, :], stack_right(pad_ref[:, first:last]))


def halo_add(int_ref, fh_ref, pad_ref, rate_ref, along_x, along_y, strided=False):
    x_low, x_high = [terms(fh_ref, pad_ref, face) for face in (0, 1)] if along_x else (None, None)
    y_low, y_high = [terms(fh_ref, pad_ref, face) for face in (2, 3)] if along_y else (None, None)
    for x in range(CX):
        for y in range(CY):
            r = x * CY + y
            total = int_ref[:, block(r)]
            if along_x and x == 0:
                total += x_low[:, block(y)]
            if along_x and x == CX - 1:
                total += x_high[:, block(y)]
            if along_y and y == 0:
                total += y_low[:, block(x)]
            if along_y and y == CY - 1:
                total += y_high[:, block(x)]
            if strided:
                rate_ref[pl.ds(r, 27, stride=32), :] = total[0:27]
            else:
                rate_ref[:, block(r)] = total


def x_faces(v_ref, xlo_ref, xhi_ref, first=0):
    for y in range(CY):
        xlo_ref[pl.ds(first + y, 9, stride=8), :] = v_ref[0:9, block(y)]
        xhi_ref[pl.ds(first + y, 9, stride=8), :] = v_ref[18:27, block(24 + y)]


def y_faces(v_ref, ylo_ref, yhi_ref):
    for x in range(CX):
        for a in range(3):
            ylo_ref[pl.ds(12 * a + x, 3, stride=4), :] = v_ref[9 * a:9 * a + 3, block(8 * x)]
            yhi_ref[pl.ds(12 * a + x, 3, stride=4), :] = v_ref[9 * a + 6:9 * a + 9, block(8 * x + 7)]


def y_first_kernel(
    int_ref, u_ref, v_ref, fh_ref, yl_ref, yh_ref, rate_ref, xlo_ref, xhi_ref, pad_ref,
):
    pad_ref[...] = jnp.zeros((16, 3072), F32)
    halo_y(yl_ref, yh_ref, pad_ref)
    halo_add(int_ref, fh_ref, pad_ref, rate_ref, False, True)
    x_faces(v_ref, xlo_ref, xhi_ref)
    for y in range(CY):
        xlo_ref[pl.ds(72 + y, 9, stride=8), :] = u_ref[0:9, block(y)] + rate_ref[0:9, block(y)]
        xhi_ref[pl.ds(72 + y, 9, stride=8), :] = (
            u_ref[18:27, block(24 + y)] + rate_ref[18:27, block(24 + y)]
        )


def x_first_kernel(
    int_ref, mid_ref, u_ref, u_mid_ref, fm_ref, fm_mid_ref, v_ref, fh_ref, xl_ref, xh_ref,
    next_ref, rate_ref, beside_ref, f_ref, ylo_ref, yhi_ref, pad_ref, own_ref,
):
    pad_ref[...] = jnp.zeros((16, 3072), F32)
    halo_x(xl_ref, xh_ref, pad_ref)
    halo_add(int_ref, fh_ref, pad_ref, rate_ref, True, False)
    rate_ref[:, 1024:3072] += mid_ref[...]
    for x in range(CX):
        cols = slice(x * 1024, (x + 1) * 1024)
        inner = slice((x - 1) * 1024, x * 1024)
        u = u_mid_ref[:, inner] if x in (1, 2) else u_ref[:, cols]
        next_ref[:, cols] = u + rate_ref[:, cols]
        f_ref[:, cols] = fm_mid_ref[:, inner] if x in (1, 2) else fm_ref[:, cols]
    y_faces(next_ref, ylo_ref, yhi_ref)
    own_ref[...] = jnp.zeros((16, 2048), F32)
    own_ref[0:9, 0:1024] = v_ref[0:9, 0:1024]
    own_ref[0:9, 1024:2048] = v_ref[18:27, 3072:4096]
    to_low = dot(fh_ref[32:64, :], stack_right(own_ref[:, 0:1024]))
    to_high = dot(fh_ref[0:32, :], stack_right(own_ref[:, 1024:2048]))
    low, high = inside("gx")
    halo_x(xl_ref, xh_ref, pad_ref, 72)
    beside_ref[...] = jnp.zeros((16, 2048), F32)
    beside_ref[0:9, 0:1024] = pad_ref[0:9, 0:1024] + jnp.where(low, to_low[18:27], 0.0)
    beside_ref[0:9, 1024:2048] = pad_ref[0:9, 1024:2048] + jnp.where(high, to_high[0:9], 0.0)


def second_kernel(
    int_ref, u_ref, fh_ref, yl_ref, yh_ref,
    v_ref, rate_ref, xlo_ref, xhi_ref, ylo_ref, yhi_ref, pad_ref,
):
    pad_ref[...] = jnp.zeros((16, 3072), F32)
    halo_y(yl_ref, yh_ref, pad_ref)
    halo_add(int_ref, fh_ref, pad_ref, rate_ref, False, True)
    v_ref[...] = u_ref[...] + 0.25 * rate_ref[...]
    x_faces(v_ref, xlo_ref, xhi_ref)
    y_faces(v_ref, ylo_ref, yhi_ref)


def weighted(f, q):
    return sum(f[m + 3:m + 4] * q[32 * m:32 * m + 32] for m in range(4))


def between_one(
    v0_ref, v1_ref, r_ref, beside_ref, c2_ref, fm_ref, wg_ref, fh_ref, pp_ref,
    int_ref, u_ref, g_ref,
):
    interior(v1_ref, wg_ref, g_ref, int_ref)
    int_ref[:, 0:1024] += terms(fh_ref, beside_ref, 0)
    int_ref[:, 3072:4096] += terms(fh_ref, beside_ref, 1)
    for x in range(CX):
        cols = slice(x * 1024, (x + 1) * 1024)
        f = fm_ref[:, cols]
        s1 = weighted(f, dot(pp_ref[:, 0:128], stack_right(r_ref[:, cols])))
        bulk = 0.75 * v0_ref[:, cols] + 0.25 * v1_ref[:, cols]
        u_ref[:, cols] = jnp.where(f[3:4] > 0.0, c2_ref[:, cols] + 0.25 * s1, bulk)


def between_two(
    v0_ref, v2_ref, r0_ref, r1_ref, c3_ref, fm_ref, live_ref, idx_ref, wg_ref, pp_ref, b3_ref, w_ref,
    u_ref, slots_ref, g_ref, int_ref,
):
    interior(v2_ref, wg_ref, g_ref, int_ref)
    for x in range(CX):
        cols = slice(x * 1024, (x + 1) * 1024)
        both = jnp.concatenate([stack_right(r1_ref[:, cols]), stack_right(r0_ref[:, cols])], axis=0)
        f = fm_ref[:, cols]
        s1 = weighted(f, dot(pp_ref[...], both))
        bulk = (1.0 / 3.0) * v0_ref[:, cols] + (2.0 / 3.0) * v2_ref[:, cols]
        old = jnp.where(f[3:4] > 0.0, c3_ref[:, cols] + (1.0 / 6.0) * s1, bulk)
        u_ref[:, cols] = old + (2.0 / 3.0) * int_ref[:, cols]
    idx = idx_ref[...]
    hot = lane_hot(idx)
    both = jnp.concatenate(
        [stack_right(to_slots(r1_ref, hot, idx)), stack_right(to_slots(r0_ref, hot, idx))], axis=0
    )
    inner = (2.0 / 3.0) * to_slots(int_ref, hot, idx)
    live = live_ref[...] > 0.0
    for m in range(4):
        value = b3_ref[m] + inner + (1.0 / 6.0) * dot(pp_ref[32 * m:32 * m + 32, :], both)
        slots_ref[:, m, :] = jnp.where(live, value[0:27], w_ref[:, m, :])


def faces_to_slots(pad_ref, idx):
    parts = []
    for g in range(8):
        parts += halves(pad_ref[:, g * GROUP:(g + 1) * GROUP])
    for x in range(CX):
        low, high = pad_ref[:, block(16 + x)], pad_ref[:, block(20 + x)]
        parts += halves(jnp.concatenate([low, high], axis=1))
    taken = dot(jnp.concatenate(parts, axis=0), lane_hot(idx))
    taken = [taken[32 * k:32 * k + 16] + taken[32 * k + 16:32 * k + 32] for k in range(12)]
    group = lax.shift_right_logical(idx, 8)
    x, y = lax.shift_right_logical(idx, 10), lax.shift_right_logical(idx, 7) & 7
    x_low = x_high = beside = jnp.zeros((16, SLOTS), F32)
    for k in range(4):
        x_low = jnp.where(group == k, taken[k], x_low)
        x_high = jnp.where(group == 12 + k, taken[4 + k], x_high)
        beside = jnp.where(x == k, taken[8 + k], beside)
    y_low, y_high = jnp.where(y == 0, beside, 0.0), jnp.where(y == CY - 1, beside, 0.0)
    return jnp.concatenate([x_low, x_high, y_low, y_high], axis=0)


def last_kernel(
    live_ref, u_ref, fh_ref, fs_ref, yl_ref, yh_ref, xl_ref, xh_ref, idx_ref, slots_ref,
    field_hbm, out_hbm, pad_ref, field_ref, out_ref, sems,
):
    pad_ref[...] = jnp.zeros((16, 3072), F32)
    halo_x(xl_ref, xh_ref, pad_ref)
    halo_y(yl_ref, yh_ref, pad_ref)
    pad_ref[...] = (2.0 / 3.0) * pad_ref[...]
    halo_add(u_ref, fh_ref, pad_ref, field_ref, True, True, strided=True)
    field_copy = pltpu.make_async_copy(field_ref, field_hbm, sems.at[0])
    field_copy.start()
    added = dot(fs_ref[...], stack_right(faces_to_slots(pad_ref, idx_ref[...])))
    added = jnp.where(live_ref[...] > 0.0, added, 0.0)
    copies = [field_copy]
    for k in range(3):
        for d in range(9 * k, 9 * k + 9):
            out_ref[d] = slots_ref[d] + added[d:d + 1]
        dofs = pl.ds(9 * k, 9)
        copies.append(pltpu.make_async_copy(out_ref.at[dofs], out_hbm.at[dofs], sems.at[k + 1]))
        copies[-1].start()
    for copy in copies:
        copy.wait()


VMEM = pl.BlockSpec(memory_space=pltpu.VMEM)
ANY = pl.BlockSpec(memory_space=pl.ANY)
HBM = pl.BlockSpec(memory_space=pltpu.HBM)
DENSE = jax.ShapeDtypeStruct((32, ZONES), F32)
X_FACES = [jax.ShapeDtypeStruct((72, 128), F32)] * 2
X_TWICE = [jax.ShapeDtypeStruct((144, 128), F32)] * 2
Y_FACES = [jax.ShapeDtypeStruct((36, 128), F32)] * 2
SLOT3 = jax.ShapeDtypeStruct((4, 32, SLOTS), F32)


def call(kernel, outs, args, scratch=(), flops=0, in_spec=VMEM, out_spec=VMEM):
    moved = 4 * sum(int(np.prod(a.shape)) for a in list(args) + list(outs))
    return pl.pallas_call(
        kernel,
        out_shape=outs,
        in_specs=[in_spec] * len(args),
        out_specs=[out_spec] * len(outs),
        scratch_shapes=list(scratch),
        compiler_params=pltpu.CompilerParams(vmem_limit_bytes=48 * 1024 * 1024),
        cost_estimate=pl.CostEstimate(flops=flops, bytes_accessed=moved, transcendentals=0),
    )(*args)


def exchange_x(low, high):
    n = lax.axis_size("gx")
    below = lax.ppermute(high, "gx", [(i, i + 1) for i in range(n - 1)])
    above = lax.ppermute(low, "gx", [(i + 1, i) for i in range(n - 1)])
    return below, above


def exchange_y(low, high):
    n = lax.axis_size("yz")
    below = lax.ppermute(high, "yz", [(i, (i + 1) % n) for i in range(n)])
    above = lax.ppermute(low, "yz", [(i, (i - 1) % n) for i in range(n)])
    return below, above


def on_device(
    state, mix_weights, mix_frac, mix_index, mix_count, vol_matrix, face_matrix, mat_matrix
):
    flat = state.reshape(27 * ROWS, CZ)
    small = [
        mix_weights.reshape(4, 27, SLOTS).transpose(1, 0, 2),
        mix_frac.reshape(4, SLOTS),
        mix_index.reshape(1, SLOTS),
        vol_matrix,
        face_matrix,
        mat_matrix.transpose(1, 0, 2),
        jnp.asarray(selections()),
    ]
    slot = lax.broadcasted_iota(jnp.int32, (1, SLOTS), 1)
    live = jnp.where(slot < mix_count.reshape(1, 1), 1.0, 0.0)
    g_space = pltpu.VMEM((224, ZONES), F32)
    pad = pltpu.VMEM((16, 3072), F32)
    bf = lambda rows, lanes: jax.ShapeDtypeStruct((rows, lanes), BF16)
    f32 = lambda rows, lanes: jax.ShapeDtypeStruct((rows, lanes), F32)

    v0, *out = call(
        first_kernel,
        [DENSE] + Y_FACES + [jax.ShapeDtypeStruct(a.shape, a.dtype) for a in small],
        [pltpu.with_memory_space_constraint(a, pltpu.HBM) for a in [flat] + small],
        [pltpu.VMEM((27 * ROWS, CZ), F32), pltpu.SemaphoreType.DMA((8,))],
        in_spec=HBM,
    )
    halo = exchange_y(*out[:2])
    weights, frac, idx, *_ = small = out[2:]
    inner, u, fm, wg, fh, fs, power, first = call(
        mixed_kernel,
        [DENSE, DENSE, f32(8, ZONES), bf(224, 128), bf(128, 64), bf(32, 256), f32(128, 128),
         f32(32, SLOTS)],
        [live, v0] + small,
        [g_space, pltpu.VMEM((32, 128), F32), pltpu.VMEM((128, 128), F32),
         pltpu.VMEM((32, SLOTS), F32)],
        flops=3 * 10**9,
    )
    inner, *faces = call(
        y_first_kernel, [DENSE] + X_TWICE, [inner, u, v0, fh, *halo], [pad]
    )
    halo = exchange_x(*faces)
    c2, c3, pp, b3, mid, u_mid, fm_mid = call(
        later_kernel,
        [DENSE, DENSE, bf(128, 256), SLOT3, f32(32, 2048), f32(32, 2048), f32(8, 2048)],
        [live, faces[0], power, weights, frac, idx, v0, wg, first],
        [pltpu.VMEM((32, SLOTS), F32), g_space],
        flops=2 * 10**9,
    )
    v1, r0, beside, fm, *faces = call(
        x_first_kernel, [DENSE, DENSE, f32(16, 2048), f32(8, ZONES)] + Y_FACES,
        [inner, mid, u, u_mid, fm, fm_mid, v0, fh, *halo],
        [pad, pltpu.VMEM((16, 2048), F32)],
    )
    halo = exchange_y(*faces)
    inner, u = call(
        between_one, [DENSE, DENSE],
        [v0, v1, r0, beside, c2, fm, wg, fh, pp], [g_space], flops=2 * 10**9,
    )
    v2, r1, *faces = call(
        second_kernel, [DENSE, DENSE] + X_FACES + Y_FACES, [inner, u, fh, *halo], [pad]
    )
    x_halo = exchange_x(*faces[:2])
    y_halo = exchange_y(*faces[2:])
    u, slots = call(
        between_two, [DENSE, jax.ShapeDtypeStruct((27, 4, SLOTS), F32)],
        [v0, v2, r0, r1, c3, fm, live, idx, wg, pp, b3, weights], [g_space, pltpu.VMEM((32, ZONES), F32)],
        flops=2 * 10**9,
    )
    field, out = call(
        last_kernel,
        [jax.ShapeDtypeStruct((27 * ROWS, CZ), F32), jax.ShapeDtypeStruct((27, 4, SLOTS), F32)],
        [live, u, fh, fs, *y_halo, *x_halo, idx, slots],
        [pad, pltpu.VMEM((27 * ROWS, CZ), F32), pltpu.VMEM((27, 4, SLOTS), F32),
         pltpu.SemaphoreType.DMA((4,))],
        out_spec=ANY,
    )
    return field.reshape(state.shape), out.transpose(1, 0, 2).reshape(mix_weights.shape)


def solution(mesh):
    placed = (
        P(None, "gx", "yz", None),
        P("gx", "yz", None, None, None),
        P("gx", "yz", None, None),
        P("gx", "yz", None),
        P("gx", "yz"),
        P(),
        P(),
        P(),
    )
    return jax.shard_map(
        on_device,
        mesh=mesh,
        in_specs=placed,
        out_specs=(P(None, "gx", "yz", None), P("gx", "yz", None, None, None)),
        check_vma=False,
    )
```
